128 devices in a mesh: lat: 16 (over y, x), chan: 8 (over z, core).
Axes of the slice: x: 4, y: 4, z: 4, core: 2. Of those that a mesh axis runs over, the one named last changes fastest.
Arguments:
- atmos: bfloat16 [384, 720, 1440], P('chan', 'lat'), may hold values from -6 to 6
- sea_temp_gain: bfloat16 [384], P('chan'), may hold values from -4 to 4
- legendre_analysis: bfloat16 [256, 256, 720], P(('lat', 'chan')), may hold values from -0.21875 to 0.21875
- legendre_synthesis: bfloat16 [256, 720, 256], P(('lat', 'chan')), may hold values from -0.375 to 0.375
- spectral_mixing_weight: bfloat16 [2, 384, 384], replicated, may hold values from -0.21875 to 0.21875
- surface_flux_weight: bfloat16 [4, 384], P(None, 'chan'), may hold values from -0.3125 to 0.3125
- flux_ocean_forcing: float32 [76, 4], replicated, may hold values from -3 to 3
- ocean: bfloat16 [76, 720, 1440], P(None, 'lat', 'chan'), may hold values from -6 to 6
- ocean_tile_mask: int32 [80, 40], P('lat', 'chan'), may hold values 0 or 1
- depthwise_filter: bfloat16 [76, 1, 7, 7], replicated, may hold values from -0.875 to 0.875
- norm_gain_vector: float32 [76], replicated, may hold values from 0.5 to 1.5
- expand_matrix: bfloat16 [304, 76], replicated, may hold values from -0.625 to 0.625
- contract_matrix: bfloat16 [76, 304], replicated, may hold values from -0.3125 to 0.3125
Outputs:
- atmos_next: bfloat16 [384, 720, 1440], P('chan', 'lat')
- ocean_next: bfloat16 [76, 720, 1440], P(None, 'lat', 'chan')
The draws below stay inside these ranges and needn't reach their ends.
All inputs are finite; a program needn't handle non-finite values. No bound on the sum of `ocean_tile_mask` on one device may be relied on, other than what follows from the above.
Results may differ from the reference program's by a relative error of at most 0.015.
Values may be sent and summed in bfloat16 or wider, within the bound.
No kernel may reach another device: no remote copies, remote signals or barrier semaphores. Data moves between devices by JAX's collectives and lax.ppermute only.
A program may use at most 128 MiB of HBM per device.

```python
import math
import jax
import jax.numpy as jnp
from jax import lax

LAT = 720
LON = 1440
ATMOS_CHANNELS = 384
M = 256
L = 256
OC = 76
HID = 304
NF = 4
KER = 7
TILE_R = 9
TILE_C = 36


def touch_ends(drawn, own_key, smallest, top_value):
    index_at = [jax.random.randint(jax.random.fold_in(own_key, axis), (), 0, length) for axis, length in enumerate(drawn.shape)]
    widest = drawn.shape.index(max(drawn.shape))
    beside = index_at[:widest] + [(index_at[widest] + 1) % drawn.shape[widest]] + index_at[widest + 1:]
    return drawn.at[tuple(index_at)].set(smallest).at[tuple(beside)].set(top_value)


def block_scale(own_key, dims, pieces, smallest, high):
    loudness = 1.0
    for axis_at, shards_of in pieces:
        steps = jax.random.uniform(jax.random.fold_in(jax.random.fold_in(own_key, 6), axis_at), (shards_of,), jnp.float32, smallest / len(pieces), high / len(pieces))
        loudness = loudness * jnp.repeat(jnp.exp(steps), dims[axis_at] // shards_of).reshape((-1,) + (1,) * (len(dims) - 1 - axis_at))
    return loudness


def gaussian(key, dims, width, reach, shards=(), kind=jnp.bfloat16):
    factor_of = block_scale(key, dims, shards, -0.22, 0.18) if shards else 1.0
    values = jax.random.normal(key, dims, jnp.float32) * width * factor_of
    return jnp.minimum(jnp.maximum(values, -reach), reach).astype(kind)


def setup_inputs(seed: int = 0) -> dict:
    keys = jax.random.split(jax.random.key(seed), 14)
    atmos = gaussian(keys[0], (ATMOS_CHANNELS, LAT, LON), 1.0, 6.0, ((0, 8), (1, 16)))
    sea_temp_gain = gaussian(keys[1], (ATMOS_CHANNELS,), 0.7, 4.0, ((0, 8),))
    legendre_analysis = gaussian(keys[2], (M, L, LAT), LAT ** -0.5, 0.21875, ((0, 128),))
    legendre_synthesis = gaussian(keys[3], (M, LAT, L), L ** -0.5, 0.375, ((0, 128),))
    spectral_mixing_weight = gaussian(keys[4], (2, ATMOS_CHANNELS, ATMOS_CHANNELS), (2 * ATMOS_CHANNELS) ** -0.5, 0.21875)
    surface_flux_weight = gaussian(keys[5], (NF, ATMOS_CHANNELS), ATMOS_CHANNELS ** -0.5, 0.3125, ((1, 8),))
    flux_ocean_forcing = gaussian(keys[6], (OC, NF), NF ** -0.5, 3.0, (), jnp.float32)
    ocean = gaussian(keys[7], (OC, LAT, LON), 1.0, 6.0, ((1, 16), (2, 8)))
    ocean_tile_mask = touch_ends((jax.random.randint(keys[8], (LAT // TILE_R, LON // TILE_C), 0, 3) < 2).astype(jnp.int32), jax.random.fold_in(keys[8], 1), 0, 1)
    depthwise_filter = gaussian(keys[9], (OC, 1, KER, KER), (KER * KER) ** -0.5, 0.875)
    norm_gain_vector = jnp.clip(1.0 + 0.1 * jax.random.normal(keys[10], (OC,), jnp.float32), 0.5, 1.5)
    expand_matrix = gaussian(keys[11], (HID, OC), OC ** -0.5, 0.625)
    contract_matrix = gaussian(keys[12], (OC, HID), HID ** -0.5, 0.3125)
    return {"atmos": atmos, "sea_temp_gain": sea_temp_gain, "legendre_analysis": legendre_analysis, "legendre_synthesis": legendre_synthesis, "spectral_mixing_weight": spectral_mixing_weight, "surface_flux_weight": surface_flux_weight, "flux_ocean_forcing": flux_ocean_forcing, "ocean": ocean, "ocean_tile_mask": ocean_tile_mask, "depthwise_filter": depthwise_filter, "norm_gain_vector": norm_gain_vector, "expand_matrix": expand_matrix, "contract_matrix": contract_matrix}


def make_tables():
    product = jnp.arange(LON, dtype=jnp.int32)[:, None] * jnp.arange(M, dtype=jnp.int32)[None, :]
    angle = 2.0 * math.pi / LON * (product % LON).astype(jnp.float32)
    factor = math.sqrt(2.0 / LON)
    forward = jnp.stack([factor * jnp.cos(angle), -factor * jnp.sin(angle)], axis=2).astype(jnp.bfloat16)
    scale_back = 1.0 / math.sqrt(M)
    angle_t = angle.T
    inverse = jnp.stack([scale_back * jnp.cos(angle_t), -scale_back * jnp.sin(angle_t)], axis=1).astype(jnp.bfloat16)
    return (forward, inverse)

def ocean_block(ocean, forcing, flag, depthwise_filter, norm_gain_vector, expand_matrix, contract_matrix):
    ocean_in = (ocean.astype(jnp.float32) + forcing).astype(jnp.bfloat16)
    smooth = lax.conv_general_dilated(ocean_in.astype(jnp.float32)[None], depthwise_filter.astype(jnp.float32), (1, 1), ((KER // 2, KER // 2), (KER // 2, KER // 2)), feature_group_count=OC, precision=lax.Precision.HIGHEST)[0]
    center = lax.optimization_barrier(jnp.mean(smooth, axis=0, keepdims=True))
    spread = lax.optimization_barrier(jnp.mean((smooth - center) ** 2, axis=0, keepdims=True))
    normed = ((smooth - center) * lax.rsqrt(spread + 1e-06) * norm_gain_vector[:, None, None]).astype(jnp.bfloat16)
    flat = normed.reshape(OC, -1)
    hidden = jax.nn.gelu(jnp.dot(expand_matrix, flat, preferred_element_type=jnp.float32)).astype(jnp.bfloat16)
    branch = jnp.dot(contract_matrix, hidden, preferred_element_type=jnp.float32).reshape(ocean.shape)
    return (ocean.astype(jnp.float32) + flag[None] * (forcing + branch)).astype(jnp.bfloat16)

def reference(atmos, sea_temp_gain, legendre_analysis, legendre_synthesis, spectral_mixing_weight, surface_flux_weight, flux_ocean_forcing, ocean, ocean_tile_mask, depthwise_filter, norm_gain_vector, expand_matrix, contract_matrix):
    sea_surface_temp = ocean[0].astype(jnp.float32)
    grid_width = 16
    group_list = ATMOS_CHANNELS // grid_width
    forward, inverse = make_tables()
    forward_flat = forward.reshape(LON, M * 2)
    inverse_flat = inverse.reshape(M * 2, LON)

    def forward_block(inputs):
        atmosphere_unit, gain_unit = inputs
        forced_ocean = atmosphere_unit.astype(jnp.float32) + gain_unit.astype(jnp.float32)[:, None, None] * sea_surface_temp[None]
        rounded = forced_ocean.astype(jnp.bfloat16)
        coefs = jnp.dot(rounded.reshape(grid_width * LAT, LON), forward_flat, preferred_element_type=jnp.float32)
        return coefs.reshape(grid_width, LAT, M, 2).transpose(3, 0, 1, 2).astype(jnp.bfloat16)
    atmos_groups = atmos.reshape(group_list, grid_width, LAT, LON)
    gain_group_list = sea_temp_gain.reshape(group_list, grid_width)
    blocks = lax.map(forward_block, (atmos_groups, gain_group_list))
    fourier = blocks.transpose(4, 1, 0, 2, 3).reshape(M, 2, ATMOS_CHANNELS, LAT)
    spectrum = jnp.einsum('mkcr,mlr->mkcl', fourier.astype(jnp.float32), legendre_analysis.astype(jnp.float32)).astype(jnp.bfloat16)
    real_part = spectral_mixing_weight[0]
    imag_part = spectral_mixing_weight[1]
    coupling = jnp.stack([jnp.stack([real_part, -imag_part]), jnp.stack([imag_part, real_part])])
    mixed = jnp.einsum('jkdc,mkcl->mjdl', coupling.astype(jnp.float32), spectrum.astype(jnp.float32)).astype(jnp.bfloat16)
    synthesis = jnp.einsum('mkcl,mrl->mkcr', mixed.astype(jnp.float32), legendre_synthesis.astype(jnp.float32)).astype(jnp.bfloat16)
    back_groups = synthesis.reshape(M, 2, group_list, grid_width, LAT).transpose(2, 3, 4, 0, 1)

    def inverse_block(inputs):
        atmosphere_unit, gain_unit, back_block = inputs
        forced_ocean = atmosphere_unit.astype(jnp.float32) + gain_unit.astype(jnp.float32)[:, None, None] * sea_surface_temp[None]
        wave_field = jnp.dot(back_block.reshape(grid_width * LAT, M * 2), inverse_flat, preferred_element_type=jnp.float32).reshape(grid_width, LAT, LON)
        return (forced_ocean + wave_field).astype(jnp.bfloat16)
    atmos_next = lax.map(inverse_block, (atmos_groups, gain_group_list, back_groups)).reshape(ATMOS_CHANNELS, LAT, LON)
    flux = jnp.dot(surface_flux_weight, atmos.reshape(ATMOS_CHANNELS, LAT * LON), preferred_element_type=jnp.float32)
    forcing = jnp.dot(flux_ocean_forcing, flux, precision=lax.Precision.HIGHEST).reshape(OC, LAT, LON)
    tile_rows = LAT // TILE_R
    tile_cols = LON // TILE_C
    flag = jnp.broadcast_to(ocean_tile_mask[:, None, :, None], (tile_rows, TILE_R, tile_cols, TILE_C)).reshape(LAT, LON).astype(jnp.float32)
    ocean_next = ocean_block(ocean, forcing, flag, depthwise_filter, norm_gain_vector, expand_matrix, contract_matrix)
    return (atmos_next, ocean_next)
```

```python
import functools
import math

import jax
import jax.numpy as jnp
import ml_dtypes
import numpy as np
from jax import lax
from jax.experimental import pallas as pl
from jax.experimental.pallas import tpu as pltpu
from jax.sharding import PartitionSpec as P

BF = jnp.bfloat16
F32 = jnp.float32
VMEM = pl.BlockSpec(memory_space=pltpu.VMEM)
NT = (((1,), (1,)), ((), ()))

HALF = 24


def peer_modes(lat_parts, chan_parts, per_dev):
    j, i, mm = np.meshgrid(np.arange(chan_parts), np.arange(lat_parts), np.arange(per_dev), indexing="ij")
    return ((i * chan_parts + j) * per_dev + mm).reshape(lat_parts * chan_parts, per_dev)


def dft_tables(lon_len, modes):
    total = modes.size
    product = np.arange(lon_len)[:, None, None] * modes.T[None]
    angle = np.float32(2.0 * math.pi / lon_len) * (product % lon_len).astype(np.float32)
    cos, sin = np.cos(angle), np.sin(angle)
    factor = np.float32(math.sqrt(2.0 / lon_len))
    forward = np.stack([factor * cos, -factor * sin], axis=2).reshape(lon_len, total * 2)
    back = np.float32(1.0 / math.sqrt(total))
    inverse = np.stack([back * cos, -back * sin], axis=2).reshape(lon_len, total * 2).T
    return forward.astype(ml_dtypes.bfloat16), np.ascontiguousarray(inverse).astype(ml_dtypes.bfloat16)


def row_swap(outer, inner):
    n = outer * inner
    swap = np.zeros((n, n), np.float32)
    o, k = np.meshgrid(np.arange(outer), np.arange(inner), indexing="ij")
    swap[(o * inner + k).ravel(), (k * outer + o).ravel()] = 1.0
    return swap.astype(ml_dtypes.bfloat16)


def dot(a, b, dims=(((1,), (0,)), ((), ()))):
    return lax.dot_general(a, b, dims, preferred_element_type=F32)


def forward_kernel(rows, x_ref, table_ref, swap_ref, out_ref, held):
    step = pl.program_id(0)
    block, ch, lon = x_ref.shape
    peers = held.shape[1]
    y = dot(x_ref[...].reshape(block * ch, lon), table_ref[...])
    row = lax.broadcasted_iota(jnp.int32, (block * ch, 1), 0)
    y = jnp.where(row < (rows - block * step) * ch, y, 0.0).astype(BF)
    for a in range(block // 2):
        pieces = [
            y[(2 * a + rh) * ch : (2 * a + rh + 1) * ch, q * peers : (q + 1) * peers]
            for rh in range(2)
            for q in range(4)
        ]
        held[step * (block // 2) + a] = jnp.concatenate(pieces, axis=0).T

    @pl.when(step == pl.num_programs(0) - 1)
    def _():
        swap = swap_ref[...]
        for at in range(0, peers, 16):
            part = held[:, at : at + 16, :].reshape(HALF * 16, held.shape[2])
            out_ref[at * HALF : (at + 16) * HALF, :] = dot(swap, part).astype(BF)


def forward(x, table, swap):
    rows, ch, lon = x.shape
    peers = table.shape[1] // 4
    block = 6
    return pl.pallas_call(
        functools.partial(forward_kernel, rows),
        out_shape=jax.ShapeDtypeStruct((peers * HALF, 8 * ch), BF),
        grid=(2 * HALF // block,),
        in_specs=[
            pl.BlockSpec((block, ch, lon), lambda g: (g, 0, 0)),
            pl.BlockSpec(table.shape, lambda g: (0, 0)),
            pl.BlockSpec(swap.shape, lambda g: (0, 0)),
        ],
        out_specs=pl.BlockSpec((peers * HALF, 8 * ch), lambda g: (0, 0)),
        scratch_shapes=[pltpu.VMEM((HALF, peers, 8 * ch), BF)],
        compiler_params=pltpu.CompilerParams(vmem_limit_bytes=40 << 20),
        cost_estimate=pl.CostEstimate(
            flops=2 * rows * ch * lon * peers * 4, bytes_accessed=14 << 20, transcendentals=0
        ),
        name="dft_forward",
    )(x, table, swap)


def spectral_kernel(
    wire_ref, analysis_ref, synthesis_ref, mix_ref, gain_ref, surface_ref, out_ref, spec, mixed
):
    size = analysis_ref.shape[2]
    wide = wire_ref.shape[1]
    pair = wide // 4
    groups = wire_ref.shape[0] // size
    surface = [
        sum(dot(surface_ref[m, rh], analysis_ref[m, rh]) for rh in range(2)) for m in range(2)
    ]
    for j in range(groups):
        turned = wire_ref[j * size : (j + 1) * size, :].T
        for m in range(2):
            total = sum(
                dot(turned[(2 * rh + m) * pair : (2 * rh + m + 1) * pair, :], analysis_ref[m, rh])
                for rh in range(2)
            )
            half = pair // 2
            gain = gain_ref[j * half : (j + 1) * half, :]
            extra = jnp.concatenate([gain * surface[m][k : k + 1, :] for k in range(2)], axis=0)
            spec[m, j * pair : (j + 1) * pair, :] = (total + extra).astype(BF)
    for m in range(2):
        mixed[m] = dot(mix_ref[...], spec[m]).astype(BF)
    for j in range(groups):
        pieces = [
            dot(synthesis_ref[m, rh], mixed[m, j * pair : (j + 1) * pair, :], NT).astype(BF)
            for rh in range(2)
            for m in range(2)
        ]
        out_ref[j * size : (j + 1) * size, :] = jnp.concatenate(pieces, axis=1)


def spectral(wire, analysis, synthesis, mix, gain, surface):
    degrees = analysis.shape[3]
    return pl.pallas_call(
        spectral_kernel,
        out_shape=jax.ShapeDtypeStruct(wire.shape, BF),
        in_specs=[VMEM] * 6,
        out_specs=VMEM,
        scratch_shapes=[pltpu.VMEM((2, mix.shape[0], degrees), BF)] * 2,
        compiler_params=pltpu.CompilerParams(vmem_limit_bytes=40 << 20),
        cost_estimate=pl.CostEstimate(flops=2 << 30, bytes_accessed=9 << 20, transcendentals=0),
        name="spectral",
    )(wire, analysis, synthesis, mix, gain, surface)


def inverse_kernel(wire_ref, table_ref, swap_ref, x_ref, gain_ref, line_ref, out_ref, held):
    step = pl.program_id(0)
    block, ch, lon = x_ref.shape
    peers = held.shape[1]

    @pl.when(step == 0)
    def _():
        swap = swap_ref[...]
        for at in range(0, peers, 16):
            part = wire_ref[at * HALF : (at + 16) * HALF, :]
            held[:, at : at + 16, :] = dot(swap, part).astype(BF).reshape(HALF, 16, held.shape[2])

    rows = []
    for a in range(block // 2):
        turned = held[step * (block // 2) + a].T
        for rh in range(2):
            rows.append(
                jnp.concatenate(
                    [turned[(4 * rh + q) * ch : (4 * rh + q + 1) * ch, :] for q in range(4)], axis=1
                )
            )
    wave = dot(jnp.concatenate(rows, axis=0), table_ref[...])
    gain = gain_ref[...]
    for a in range(block):
        forced = x_ref[a].astype(F32) + gain * line_ref[a].astype(F32)
        out_ref[a] = (forced + wave[a * ch : (a + 1) * ch, :]).astype(BF)


def inverse(wire, table, swap, x, gain, line):
    rows, ch, lon = x.shape
    peers = table.shape[0] // 4
    block = 6
    return pl.pallas_call(
        inverse_kernel,
        out_shape=jax.ShapeDtypeStruct(x.shape, BF),
        grid=(2 * HALF // block,),
        in_specs=[
            pl.BlockSpec(wire.shape, lambda g: (0, 0)),
            pl.BlockSpec(table.shape, lambda g: (0, 0)),
            pl.BlockSpec(swap.shape, lambda g: (0, 0)),
            pl.BlockSpec((block, ch, lon), lambda g: (g, 0, 0)),
            pl.BlockSpec(gain.shape, lambda g: (0, 0)),
            pl.BlockSpec((block, 1, lon), lambda g: (g, 0, 0)),
        ],
        out_specs=pl.BlockSpec((block, ch, lon), lambda g: (g, 0, 0)),
        scratch_shapes=[pltpu.VMEM((HALF, peers, 8 * ch), BF)],
        compiler_params=pltpu.CompilerParams(vmem_limit_bytes=40 << 20),
        cost_estimate=pl.CostEstimate(
            flops=2 * rows * ch * lon * peers * 4, bytes_accessed=20 << 20, transcendentals=0
        ),
        name="dft_inverse",
    )(wire, table, swap, x, gain, line)


def flux_kernel(rows, reach, x_ref, weight_ref, out_ref):
    step = pl.program_id(0)
    block, ch, lon = x_ref.shape
    peers, _, wide = out_ref.shape
    tile = lon // peers
    row = lax.broadcasted_iota(jnp.int32, (block * ch, 1), 0)
    x = x_ref[...].reshape(block * ch, lon)
    x = jnp.where(row < (rows - block * step) * ch, x, jnp.zeros_like(x))
    y = dot(weight_ref[...], x)
    zeros = jnp.zeros((y.shape[0], reach), F32)
    y = jnp.concatenate([zeros, y, zeros], axis=1)
    half = y.shape[0] // 2
    for j in range(peers):
        part = y[:, tile * j : tile * j + tile + 2 * reach]
        out_ref[j] = jnp.concatenate([part[:half], part[half:]], axis=1).astype(BF)


def flux_parts(x, weight, reach, peers):
    rows, ch, lon = x.shape
    block = 8
    steps = pl.cdiv(rows, block)
    eye = jnp.eye(block, dtype=BF)
    spread = weight.reshape(2, 1, 2, 1, ch) * eye[None, :, None, :, None]
    spread = spread.reshape(4 * block, block * ch)
    wide = 2 * (lon // peers + 2 * reach)
    return pl.pallas_call(
        functools.partial(flux_kernel, rows, reach),
        out_shape=jax.ShapeDtypeStruct((peers, steps * 2 * block, wide), BF),
        grid=(steps,),
        in_specs=[
            pl.BlockSpec((block, ch, lon), lambda g: (g, 0, 0)),
            pl.BlockSpec(spread.shape, lambda g: (0, 0)),
        ],
        out_specs=pl.BlockSpec((peers, 2 * block, wide), lambda g: (0, g, 0)),
        compiler_params=pltpu.CompilerParams(vmem_limit_bytes=24 << 20),
        cost_estimate=pl.CostEstimate(flops=1 << 30, bytes_accessed=7 << 20, transcendentals=0),
        name="flux_parts",
    )(x, spread)


def ocean_kernel(
    reach, padded_ref, flux_ref, force_ref, taps_ref, gain_ref, expand_ref, contract_ref, flag_ref,
    center_ref, out_ref, wet, taps, smooth
):
    step = pl.program_id(0)
    block, ch, cols = center_ref.shape
    total_rows, high, wide = wet.shape
    side = 2 * reach + 1
    force = [force_ref[:, f : f + 1] for f in range(4)]

    @pl.when(step == 0)
    def _():
        def fill(r, carry):
            flux = flux_ref[r]
            forcing = sum(force[f] * flux[f : f + 1, : padded_ref.shape[2]] for f in range(4))
            value = (padded_ref[r].astype(F32) + forcing).astype(BF).astype(F32)
            wet[r, :ch, : padded_ref.shape[2]] = value
            return carry

        lax.fori_loop(0, total_rows, fill, 0)
        for k in range(side * side):
            taps[k] = jnp.broadcast_to(taps_ref[:, k : k + 1], taps.shape[1:])

    start = step * block

    def channels(t, carry):
        at = pl.multiple_of(t * 8, 8)
        rows = [wet[start + d, pl.ds(at, 8), :] for d in range(block + side - 1)]
        total = [None] * block
        for dx in range(side):
            part = [None] * block
            for dy in range(side):
                tap = taps[dy * side + dx, pl.ds(at, 8), :]
                tap = jnp.concatenate([tap] * (wide // 128), axis=1)
                for b in range(block):
                    term = tap * rows[b + dy]
                    part[b] = term if part[b] is None else part[b] + term
            for b in range(block):
                moved = part[b] if dx == 0 else pltpu.roll(part[b], wide - dx, 1)
                total[b] = moved if total[b] is None else total[b] + moved
        for b in range(block):
            smooth[b, pl.ds(at, 8), :] = total[b]
        return carry

    lax.fori_loop(0, high // 8, channels, 0)
    normed = []
    for b in range(block):
        value = smooth[b, :ch, :]
        value = value - jnp.mean(value, axis=0, keepdims=True)
        spread = jnp.mean(value * value, axis=0, keepdims=True)
        normed.append((value * lax.rsqrt(spread + 1e-06) * gain_ref[...]).astype(BF))
    for b in range(block):
        hidden = jax.nn.gelu(dot(expand_ref[...], normed[b])).astype(BF)
        branch = dot(contract_ref[...], hidden)[:, :cols]
        flux = flux_ref[start + reach + b][:, reach : reach + cols]
        forcing = sum(force[f] * flux[f : f + 1, :] for f in range(4))
        flag = flag_ref[b]
        out_ref[b] = (center_ref[b].astype(F32) + flag * (forcing + branch)).astype(BF)


def ocean_block(padded, flux, force, taps, gain, expand, contract, flag, center, reach):
    rows, ch, cols = center.shape
    block = 5
    high = pl.cdiv(ch, 8) * 8
    wide = pl.cdiv(cols + 2 * reach, 128) * 128
    whole = lambda a: pl.BlockSpec(a.shape, lambda g: (0,) * a.ndim)
    return pl.pallas_call(
        functools.partial(ocean_kernel, reach),
        out_shape=jax.ShapeDtypeStruct(center.shape, BF),
        grid=(rows // block,),
        in_specs=[whole(a) for a in (padded, flux, force, taps, gain, expand, contract)]
        + [
            pl.BlockSpec((block, 1, cols), lambda g: (g, 0, 0)),
            pl.BlockSpec((block, ch, cols), lambda g: (g, 0, 0)),
        ],
        out_specs=pl.BlockSpec((block, ch, cols), lambda g: (g, 0, 0)),
        scratch_shapes=[
            pltpu.VMEM((rows + 2 * reach, high, wide), F32),
            pltpu.VMEM((taps.shape[1], high, 128), F32),
            pltpu.VMEM((block, high, wide), F32),
        ],
        compiler_params=pltpu.CompilerParams(vmem_limit_bytes=32 << 20),
        cost_estimate=pl.CostEstimate(
            flops=20 << 30, bytes_accessed=8 << 20, transcendentals=3 << 20
        ),
        name="ocean_block",
    )(padded, flux, force, taps, gain, expand, contract, flag, center)


def halo(block, axis, dim, width):
    count = lax.axis_size(axis)
    forward = [(i, i + 1) for i in range(count - 1)]
    backward = [(target, source) for source, target in forward]
    size = block.shape[dim]
    low = lax.ppermute(lax.slice_in_dim(block, size - width, size, axis=dim), axis, forward)
    high = lax.ppermute(lax.slice_in_dim(block, 0, width, axis=dim), axis, backward)
    return jnp.concatenate([low, block, high], axis=dim)


def body(
    atmos,
    sea_temp_gain,
    legendre_analysis,
    legendre_synthesis,
    spectral_mixing_weight,
    surface_flux_weight,
    flux_ocean_forcing,
    ocean,
    ocean_tile_mask,
    depthwise_filter,
    norm_gain_vector,
    expand_matrix,
    contract_matrix,
):
    lat_parts = lax.axis_size("lat")
    chan_parts = lax.axis_size("chan")
    chan_at = lax.axis_index("chan")
    ch, rows, lon = atmos.shape
    per_dev, degrees, _ = legendre_analysis.shape
    all_ch = ch * chan_parts
    ocean_ch, _, cols = ocean.shape
    reach = depthwise_filter.shape[2] // 2
    peers = lat_parts * chan_parts
    padded_rows = 2 * HALF

    table_fwd, table_inv = dft_tables(lon, peer_modes(lat_parts, chan_parts, per_dev))
    table_fwd, table_inv = jnp.asarray(table_fwd), jnp.asarray(table_inv)
    swap_out = jnp.asarray(row_swap(16, HALF))
    swap_in = jnp.asarray(row_swap(HALF, 16))

    x = jnp.transpose(atmos, (1, 0, 2))
    sea = jnp.transpose(ocean, (1, 0, 2))

    def exchange(wire):
        return lax.all_to_all(
            wire.reshape(peers, HALF, 8 * ch), ("chan", "lat"), 0, 0, tiled=True
        ).reshape(wire.shape)

    own = jnp.pad(sea[:, 0, :], ((0, 3), (0, 0)))
    own = own.at[rows, :ch].set(sea_temp_gain)
    lines = lax.all_to_all(
        jnp.broadcast_to(own[None], (chan_parts,) + own.shape), "chan", 0, 0, tiled=True
    )
    all_gain = lines[:, rows, :ch].reshape(all_ch)
    line = jnp.transpose(lines[:, :rows], (1, 0, 2)).reshape(rows, lon)

    wire = forward(x, table_fwd, swap_out)
    gathered = exchange(wire)

    surface = dot(line, table_fwd).reshape(rows, 4, chan_parts, lat_parts)
    surface = lax.dynamic_index_in_dim(surface, chan_at, axis=2, keepdims=False).astype(BF)
    surface = jnp.pad(jnp.transpose(surface, (2, 1, 0)), ((0, 0), (0, 0), (0, padded_rows - rows)))
    surface = lax.all_to_all(surface, "lat", 0, 0, tiled=True)
    surface = surface.reshape(lat_parts, 2, 2, HALF, 2).transpose(1, 4, 2, 0, 3)
    surface = surface.reshape(2, 2, 2, lat_parts * HALF)

    def banded(table):
        table = table.reshape(per_dev, lat_parts, rows, degrees)
        table = jnp.pad(table, ((0, 0), (0, 0), (0, padded_rows - rows), (0, 0)))
        table = table.reshape(per_dev, lat_parts, HALF, 2, degrees).transpose(0, 3, 1, 2, 4)
        return table.reshape(per_dev, 2, lat_parts * HALF, degrees)

    analysis = banded(jnp.transpose(legendre_analysis, (0, 2, 1)))
    synthesis = banded(legendre_synthesis)
    real_part, imag_part = spectral_mixing_weight[0], spectral_mixing_weight[1]
    mix = jnp.stack([jnp.stack([real_part, -imag_part]), jnp.stack([imag_part, real_part])])
    mix = mix.reshape(2, 2, chan_parts, ch, chan_parts, ch).transpose(2, 0, 3, 4, 1, 5)
    mix = mix.reshape(2 * all_ch, 2 * all_ch)
    returned = exchange(
        spectral(gathered, analysis, synthesis, mix, all_gain.astype(F32)[:, None], surface)
    )

    parts = lax.all_to_all(
        flux_parts(x, surface_flux_weight, reach, chan_parts), "chan", 0, 0, tiled=True
    )
    flux = jnp.sum(parts.astype(F32), axis=0)[: 2 * rows]
    flux = halo(flux, "lat", 0, 2 * reach)
    flux = flux.reshape(rows + 2 * reach, 2, 2, cols + 2 * reach).transpose(0, 2, 1, 3)
    flux = flux.reshape(rows + 2 * reach, 4, cols + 2 * reach)
    padded = halo(halo(sea, "lat", 0, reach), "chan", 2, reach)
    tile_rows, tile_cols = ocean_tile_mask.shape
    flag = jnp.repeat(jnp.repeat(ocean_tile_mask, rows // tile_rows, 0), cols // tile_cols, 1)
    taps = depthwise_filter.reshape(ocean_ch, -1).astype(F32)
    taps = jnp.pad(taps, ((0, -ocean_ch % 8), (0, 0)))
    ocean_next = ocean_block(
        padded,
        flux,
        flux_ocean_forcing,
        taps,
        norm_gain_vector[:, None],
        expand_matrix,
        contract_matrix,
        flag.astype(F32)[:, None, :],
        sea,
        reach,
    )

    atmos_next = inverse(
        returned, table_inv, swap_in, x, sea_temp_gain.astype(F32)[:, None], line[:, None, :]
    )
    return (jnp.transpose(atmos_next, (1, 0, 2)), jnp.transpose(ocean_next, (1, 0, 2)))


def solution(mesh):
    in_specs = (
        P("chan", "lat", None),
        P("chan"),
        P(("lat", "chan"), None, None),
        P(("lat", "chan"), None, None),
        P(),
        P(None, "chan"),
        P(),
        P(None, "lat", "chan"),
        P("lat", "chan"),
        P(),
        P(),
        P(),
        P(),
    )
    out_specs = (P("chan", "lat", None), P(None, "lat", "chan"))
    return jax.shard_map(body, mesh=mesh, in_specs=in_specs, out_specs=out_specs, check_vma=False)
```

```python
import functools
import math

import jax
import jax.numpy as jnp
import ml_dtypes
import numpy as np
from jax import lax
from jax.experimental import pallas as pl
from jax.experimental.pallas import tpu as pltpu
from jax.sharding import PartitionSpec as P

BF = jnp.bfloat16
F32 = jnp.float32
VMEM = pl.BlockSpec(memory_space=pltpu.VMEM)
NT = (((1,), (1,)), ((), ()))

HALF = 24


def peer_modes(lat_parts, chan_parts, per_dev):
    j, i, mm = np.meshgrid(np.arange(chan_parts), np.arange(lat_parts), np.arange(per_dev), indexing="ij")
    return ((i * chan_parts + j) * per_dev + mm).reshape(lat_parts * chan_parts, per_dev)


def dft_tables(lon_len, modes):
    total = modes.size
    product = np.arange(lon_len)[:, None, None] * modes.T[None]
    angle = np.float32(2.0 * math.pi / lon_len) * (product % lon_len).astype(np.float32)
    cos, sin = np.cos(angle), np.sin(angle)
    factor = np.float32(math.sqrt(2.0 / lon_len))
    forward = np.stack([factor * cos, -factor * sin], axis=2).reshape(lon_len, total * 2)
    back = np.float32(1.0 / math.sqrt(total))
    inverse = np.stack([back * cos, -back * sin], axis=2).reshape(lon_len, total * 2).T
    return forward.astype(ml_dtypes.bfloat16), np.ascontiguousarray(inverse).astype(ml_dtypes.bfloat16)


def row_swap(outer, inner):
    n = outer * inner
    swap = np.zeros((n, n), np.float32)
    o, k = np.meshgrid(np.arange(outer), np.arange(inner), indexing="ij")
    swap[(o * inner + k).ravel(), (k * outer + o).ravel()] = 1.0
    return swap.astype(ml_dtypes.bfloat16)


def dot(a, b, dims=(((1,), (0,)), ((), ()))):
    return lax.dot_general(a, b, dims, preferred_element_type=F32)


ANY = pl.BlockSpec(memory_space=pl.ANY)
SMEM = pl.BlockSpec(memory_space=pltpu.SMEM)
HBM = pl.BlockSpec(memory_space=pltpu.HBM)
BLOCK = 6


def row_groups(rows):
    return [(at, min(BLOCK, rows - at)) for at in range(0, rows, BLOCK)]


def column(row_ref):
    n = row_ref.shape[1]
    rows = jnp.broadcast_to(row_ref[...].astype(F32), (16, n))
    first = lax.broadcasted_iota(jnp.int32, (16, 128), 0) == 0
    return dot(rows.astype(BF), first.astype(F32).astype(BF), (((0,), (0,)), ((), ())))


def forward_kernel(
    at_ref, x, sea_ref, gain_ref, table, swap_ref, out_ref, sea, held, out, out_sems, sems
):
    rows, ch, lon = x.shape
    peers = held.shape[1]
    groups = row_groups(rows)
    sea_copy = pltpu.make_async_copy(sea_ref.at[:, pl.ds(0, 16), :], sea, sems.at[0])
    sea_copy.start()
    for at, size in groups:
        y = dot(x[at : at + size].reshape(size * ch, lon), table[...]).astype(BF)
        for a in range(0, size, 2):
            pieces = []
            for rh in range(2):
                for q in range(4):
                    if a + rh < size:
                        pieces.append(y[(a + rh) * ch : (a + rh + 1) * ch, q * peers : (q + 1) * peers])
                    else:
                        pieces.append(jnp.zeros((ch, peers), BF))
            held[(at + a) // 2] = jnp.concatenate(pieces, axis=0).T

    sea_copy.wait()
    own = sea[:, 0, :].astype(F32)
    own = jnp.concatenate([own, jnp.zeros((ch - rows, own.shape[1]), F32)], axis=0)
    wide = pl.cdiv(lon, 128) * 128
    own = jnp.concatenate([own, jnp.zeros((ch, wide - own.shape[1]), F32)], axis=1)
    own = pltpu.roll(own, at_ref[0], 1)[:, :lon].astype(BF)
    y = dot(own, table[...]).astype(BF)
    pieces = [y[:, q * peers : (q + 1) * peers] for q in range(4)]
    pieces.append(column(gain_ref).astype(BF))
    pieces.append(jnp.zeros((3 * ch, peers), BF))
    held[HALF - 1] = jnp.concatenate(pieces, axis=0).T

    out_copies = []
    for b in range(peers // 16):
        part = held[:, b * 16 : (b + 1) * 16, :].reshape(HALF * 16, held.shape[2])
        span = pl.ds(b * 16 * HALF, 16 * HALF)
        out[span, :] = dot(swap_ref[...], part).astype(BF)
        out_copies.append(pltpu.make_async_copy(out.at[span], out_ref.at[span], out_sems.at[b]))
        out_copies[-1].start()
    for copy in out_copies:
        copy.wait()


def forward(at, x, sea, gain, table, swap):
    rows, ch, lon = x.shape
    peers = table.shape[1] // 4
    return pl.pallas_call(
        forward_kernel,
        out_shape=pltpu.HBM((peers * HALF, 8 * ch), BF),
        in_specs=[SMEM, VMEM, HBM, VMEM, VMEM, VMEM],
        out_specs=ANY,
        scratch_shapes=[
            pltpu.VMEM((rows, 16, sea.shape[2]), BF),
            pltpu.VMEM((HALF, peers, 8 * ch), BF),
            pltpu.VMEM((peers * HALF, 8 * ch), BF),
            pltpu.SemaphoreType.DMA((peers // 16,)),
            pltpu.SemaphoreType.DMA((1,)),
        ],
        compiler_params=pltpu.CompilerParams(vmem_limit_bytes=24 << 20),
        cost_estimate=pl.CostEstimate(
            flops=2 * rows * ch * lon * peers * 4, bytes_accessed=14 << 20, transcendentals=0
        ),
        name="dft_forward",
    )(at, x, sea, gain, table, swap)


def spread_last(lat_parts):
    n = lat_parts * HALF
    col = np.arange(n)
    spread = np.zeros((n, n), np.float32)
    spread[col // HALF * HALF + HALF - 1, col] = 1.0
    return spread.astype(ml_dtypes.bfloat16)


def spectral_kernel(
    wire_hbm, analysis_hbm, synthesis_hbm, mix_hbm, spread_hbm, out_ref,
    wire_ref, analysis_ref, synthesis_ref, mix_ref, spread_ref, spec, mixed, gains, out,
    wire_sems, in_sems, sems
):
    size = analysis_ref.shape[2]
    ch = wire_ref.shape[1] // 8
    groups = wire_ref.shape[0] // size
    pairs = (
        (analysis_hbm, analysis_ref), (spread_hbm, spread_ref), (mix_hbm, mix_ref), (synthesis_hbm, synthesis_ref)
    )
    tables = [pltpu.make_async_copy(a, b, in_sems.at[k]) for k, (a, b) in enumerate(pairs)]
    wires = []
    for j in range(groups):
        span = pl.ds(j * size, size)
        wires.append(pltpu.make_async_copy(wire_hbm.at[span], wire_ref.at[span], wire_sems.at[j]))
    wires[0].start()
    tables[0].start()
    for copy in wires[1:] + tables[1:]:
        copy.start()
    tables[0].wait()
    lines = 0.0
    for j in range(groups):
        wires[j].wait()
        turned = wire_ref[j * size : (j + 1) * size, :].T
        for m in range(2):
            total = sum(
                dot(turned[(4 * rh + 2 * m) * ch : (4 * rh + 2 * m + 2) * ch, :], analysis_ref[m, rh])
                for rh in range(2)
            ).astype(BF)
            for k in range(2):
                spec[m, k, j * ch : (j + 1) * ch, :] = total[k * ch : (k + 1) * ch, :]
        gains[j * ch : (j + 1) * ch, :] = turned[4 * ch : 5 * ch, :128]
        lines = lines + turned[: 4 * ch, :].astype(F32)

    for copy in tables[1:]:
        copy.wait()
    lines = dot(lines.astype(BF), spread_ref[...])
    own_row = lax.broadcasted_iota(jnp.int32, (ch, size), 0)
    rr = lax.rem(lax.broadcasted_iota(jnp.int32, (ch, size), 1), HALF)
    real, imag = mix_ref[0], mix_ref[1]
    gain_real = dot(real, gains[...])[:, HALF - 1 : HALF]
    gain_imag = dot(imag, gains[...])[:, HALF - 1 : HALF]
    for m in range(2):
        surface = 0.0
        for rh in range(2):
            both = [
                jnp.sum(
                    jnp.where(own_row == 2 * rr + rh, lines[q * ch : (q + 1) * ch, :], 0.0),
                    axis=0,
                    keepdims=True,
                )
                for q in (2 * m, 2 * m + 1)
            ]
            both.append(jnp.zeros((6, size), F32))
            both = jnp.concatenate(both, axis=0).astype(BF)
            surface = surface + dot(both, analysis_ref[m, rh])
        sr, si = surface[0:1, :], surface[1:2, :]
        value = dot(real, spec[m, 0]) - dot(imag, spec[m, 1])
        mixed[m, 0] = (value + (gain_real * sr - gain_imag * si)).astype(BF)
        value = dot(imag, spec[m, 0]) + dot(real, spec[m, 1])
        mixed[m, 1] = (value + (gain_imag * sr + gain_real * si)).astype(BF)

    copies = []
    for j in range(groups):
        pieces = []
        for rh in range(2):
            for m in range(2):
                both = [mixed[m, k, j * ch : (j + 1) * ch, :] for k in range(2)]
                pieces.append(dot(synthesis_ref[m, rh], jnp.concatenate(both, axis=0), NT).astype(BF))
        span = pl.ds(j * size, size)
        out[span, :] = jnp.concatenate(pieces, axis=1)
        copies.append(pltpu.make_async_copy(out.at[span], out_ref.at[span], sems.at[j]))
        copies[-1].start()
    for copy in copies:
        copy.wait()


def spectral(wire, analysis, synthesis, mix, spread):
    _, _, size, degrees = analysis.shape
    groups = wire.shape[0] // size
    all_ch = mix.shape[1]
    return pl.pallas_call(
        spectral_kernel,
        out_shape=pltpu.HBM(wire.shape, BF),
        in_specs=[ANY] * 5,
        out_specs=ANY,
        scratch_shapes=[
            *(pltpu.VMEM(a.shape, BF) for a in (wire, analysis, synthesis, mix, spread)),
            pltpu.VMEM((2, 2, all_ch, degrees), BF),
            pltpu.VMEM((2, 2, all_ch, degrees), BF),
            pltpu.VMEM((all_ch, 128), BF),
            pltpu.VMEM(wire.shape, BF),
            pltpu.SemaphoreType.DMA((groups,)),
            pltpu.SemaphoreType.DMA((4,)),
            pltpu.SemaphoreType.DMA((groups,)),
        ],
        compiler_params=pltpu.CompilerParams(vmem_limit_bytes=56 << 20),
        cost_estimate=pl.CostEstimate(flops=2 << 30, bytes_accessed=9 << 20, transcendentals=0),
        name="spectral",
    )(wire, analysis, synthesis, mix, spread)


def inverse_kernel(
    wire_ref, table_ref, swap_ref, x_ref, gain_ref, parts_ref, out_ref,
    wire, table, held, x, out, lines, wire_sems, x_sems, out_sems, sems
):
    rows, ch, lon = x.shape
    peers = held.shape[1]
    groups = row_groups(rows)
    wire_copies = []
    for b in range(peers // 16):
        span = pl.ds(b * 16 * HALF, 16 * HALF)
        wire_copies.append(pltpu.make_async_copy(wire_ref.at[span], wire.at[span], wire_sems.at[b]))
        wire_copies[-1].start()
    table_copy = pltpu.make_async_copy(table_ref, table, sems.at[0])
    table_copy.start()
    x_copies = []
    for g, (at, size) in enumerate(groups):
        span = pl.ds(at, size)
        x_copies.append(pltpu.make_async_copy(x_ref.at[span], x.at[span], x_sems.at[g]))
        x_copies[-1].start()
    for b in range(peers // 16):
        wire_copies[b].wait()
        part = dot(swap_ref[...], wire[b * 16 * HALF : (b + 1) * 16 * HALF, :]).astype(BF)
        held[:, b * 16 : (b + 1) * 16, :] = part.reshape(HALF, 16, held.shape[2])
    chans, end, _ = parts_ref.shape
    for half in range(2):
        lines[half] = jnp.concatenate(
            [
                parts_ref[j, end - 32 :, half * PITCH : half * PITCH + lon // chans].astype(F32)
                for j in range(chans)
            ],
            axis=1,
        )
    gain = column(gain_ref)[:, :1]
    table_copy.wait()

    def wave_of(at, size):
        waves = []
        for a in range(0, size, 2):
            turned = held[(at + a) // 2].T
            for rh in range(min(2, size - a)):
                parts = [turned[(4 * rh + q) * ch : (4 * rh + q + 1) * ch, :] for q in range(4)]
                waves.append(jnp.concatenate(parts, axis=1))
        return dot(jnp.concatenate(waves, axis=0), table[...])

    out_copies = []
    wave = wave_of(*groups[0])
    for g, (at, size) in enumerate(groups):
        x_copies[g].wait()
        later = wave_of(*groups[g + 1]) if g + 1 < len(groups) else None
        for a in range(size):
            line = lines[a % 2, (at + a) // 2 : (at + a) // 2 + 1, :]
            forced = x[at + a].astype(F32) + gain * line
            out[at + a] = (forced + wave[a * ch : (a + 1) * ch, :]).astype(BF)
        span = pl.ds(at, size)
        out_copies.append(pltpu.make_async_copy(out.at[span], out_ref.at[span], out_sems.at[g]))
        out_copies[-1].start()
        wave = later
    for copy in out_copies:
        copy.wait()


def inverse(wire, table, swap, x, gain, parts):
    rows, ch, lon = x.shape
    peers = table.shape[0] // 4
    groups = len(row_groups(rows))
    return pl.pallas_call(
        inverse_kernel,
        out_shape=pltpu.HBM(x.shape, BF),
        in_specs=[ANY, ANY, VMEM, ANY, VMEM, VMEM],
        out_specs=ANY,
        scratch_shapes=[
            pltpu.VMEM(wire.shape, BF),
            pltpu.VMEM(table.shape, BF),
            pltpu.VMEM((HALF, peers, 8 * ch), BF),
            pltpu.VMEM(x.shape, BF),
            pltpu.VMEM(x.shape, BF),
            pltpu.VMEM((2, 32, lon), F32),
            pltpu.SemaphoreType.DMA((peers // 16,)),
            pltpu.SemaphoreType.DMA((groups,)),
            pltpu.SemaphoreType.DMA((groups,)),
            pltpu.SemaphoreType.DMA((1,)),
        ],
        compiler_params=pltpu.CompilerParams(vmem_limit_bytes=56 << 20),
        cost_estimate=pl.CostEstimate(
            flops=2 * rows * ch * lon * peers * 4, bytes_accessed=20 << 20, transcendentals=0
        ),
        name="dft_inverse",
    )(wire, table, swap, x, gain, parts)


PITCH = 192


def flux_kernel(reach, x_ref, sea_ref, weight_ref, out_ref, x, sea, x_sems, sems):
    rows, ch, lon = x.shape
    peers = out_ref.shape[0]
    tile = lon // peers
    block = 8
    groups = [(at, min(block, rows - at)) for at in range(0, rows, block)]
    copies = []
    for g, (at, size) in enumerate(groups):
        span = pl.ds(at, size)
        copies.append(pltpu.make_async_copy(x_ref.at[span], x.at[span], x_sems.at[g]))
        copies[-1].start()
    sea_copy = pltpu.make_async_copy(sea_ref.at[:, pl.ds(0, 16), :], sea, sems.at[0])
    sea_copy.start()
    weight = weight_ref[...].astype(F32)
    weight = jnp.concatenate([weight] * block, axis=1)
    weight = jnp.concatenate([weight] * block, axis=0)
    row = lax.broadcasted_iota(jnp.int32, weight.shape, 0)
    col = lax.broadcasted_iota(jnp.int32, weight.shape, 1)
    keep = col // ch == row % 16 // 4 * 2 + row // 16
    weight = jnp.where(keep, weight, 0.0).astype(BF)
    before = jnp.zeros((4 * block, reach), F32)
    after = jnp.zeros((4 * block, PITCH - tile - reach), F32)
    for g, (at, size) in enumerate(groups):
        copies[g].wait()
        y = dot(weight[:, : size * ch], x[at : at + size].reshape(size * ch, lon))
        y = jnp.concatenate([before, y, after], axis=1)
        for j in range(peers):
            part = y[:, tile * j : tile * j + PITCH]
            part = jnp.concatenate([part[: 2 * block], part[2 * block :]], axis=1)
            out_ref[j, 2 * block * g : 2 * block * (g + 1), :] = part.astype(BF)
    sea_copy.wait()
    own = jnp.concatenate([sea[:, 0, :].astype(F32), jnp.zeros((ch - rows, tile), F32)], axis=0)
    halves = []
    for half in range(2):
        pick = lax.broadcasted_iota(jnp.int32, (32, ch), 1) == (
            2 * lax.broadcasted_iota(jnp.int32, (32, ch), 0) + half
        )
        halves.append(dot(pick.astype(F32).astype(BF), own.astype(BF)))
        halves.append(jnp.zeros((32, PITCH - tile), F32))
    own = jnp.concatenate(halves, axis=1).astype(BF)
    for j in range(peers):
        out_ref[j, out_ref.shape[1] - 32 :, :] = own


def flux_parts(x, sea, weight, reach, peers):
    rows, ch, lon = x.shape
    groups = pl.cdiv(rows, 8)
    return pl.pallas_call(
        functools.partial(flux_kernel, reach),
        out_shape=jax.ShapeDtypeStruct((peers, groups * 16 + 32, 2 * PITCH), BF),
        in_specs=[HBM, HBM, VMEM],
        out_specs=VMEM,
        scratch_shapes=[
            pltpu.VMEM(x.shape, BF),
            pltpu.VMEM((rows, 16, sea.shape[2]), BF),
            pltpu.SemaphoreType.DMA((groups,)),
            pltpu.SemaphoreType.DMA((1,)),
        ],
        compiler_params=pltpu.CompilerParams(vmem_limit_bytes=24 << 20),
        cost_estimate=pl.CostEstimate(flops=1 << 30, bytes_accessed=7 << 20, transcendentals=0),
        name="flux_parts",
    )(x, sea, weight)


def column_kernel(reach, center_ref, first_ref, last_ref):
    rows, ch, cols = center_ref.shape
    shape = (16, cols)
    row = lax.broadcasted_iota(jnp.int32, shape, 0)
    col = lax.broadcasted_iota(jnp.int32, shape, 1)
    want = jnp.where(row % 8 < 2 * reach, row % 8 % reach + row // 8 * (cols - reach), -1)
    picks = []
    for half in range(2):
        pick = (col == want) & (row % 8 // reach == half)
        picks.append(pick.astype(F32).astype(BF))
    for s in range((rows + 1) // 2):
        value = dot(picks[0], center_ref[2 * s], NT)
        if 2 * s + 1 < rows:
            value = value + dot(picks[1], center_ref[2 * s + 1], NT)
        first_ref[s] = value[:8].astype(BF)
        last_ref[s] = value[8:].astype(BF)


def edge_columns(center, reach):
    rows, ch, _ = center.shape
    out = jax.ShapeDtypeStruct(((rows + 1) // 2, 8, ch), BF)
    return pl.pallas_call(
        functools.partial(column_kernel, reach),
        out_shape=(out, out),
        in_specs=[VMEM],
        out_specs=(VMEM, VMEM),
        compiler_params=pltpu.CompilerParams(vmem_limit_bytes=16 << 20),
        cost_estimate=pl.CostEstimate(flops=1 << 20, bytes_accessed=1 << 20, transcendentals=0),
        name="edge_columns",
    )(center)


def edge_picks(reach, span):
    picks = np.zeros((16, 2 * PITCH), np.float32)
    for side in range(2):
        for half in range(2):
            for dx in range(reach):
                picks[8 * side + reach * half + dx, PITCH * half + side * (span - reach) + dx] = 1.0
    return picks.astype(ml_dtypes.bfloat16)


def pair_forcing(s, left_ref, right_ref, picks, flux, force):
    high = flux.astype(BF).astype(F32)
    low = flux - high
    flux = jnp.concatenate([high, low, high, jnp.zeros_like(high)], axis=0).astype(BF)
    edge = jnp.concatenate([left_ref[s].astype(F32), right_ref[s].astype(F32)], axis=0).astype(BF)
    return dot(
        jnp.concatenate([edge, force], axis=0),
        jnp.concatenate([picks, flux], axis=0),
        (((0,), (0,)), ((), ())),
    )


def pair_rows(first, second, reach):
    ch, cols = first.shape
    before = jnp.zeros((ch, reach), F32)
    after = jnp.zeros((ch, PITCH - cols - reach), F32)
    first, second = first.astype(F32), second.astype(F32)
    return jnp.concatenate([before, first, after, before, second, after], axis=1)


def wet_kernel(
    reach, center_ref, left_ref, right_ref, picks_ref, parts_ref, force_ref,
    odd_ref, even_ref, forcing_ref, first_ref, last_ref, flux
):
    rows = center_ref.shape[0]
    own_pairs = odd_ref.shape[0]
    picks, force = picks_ref[...], force_ref[...]
    total = parts_ref[0].astype(F32)
    for j in range(1, parts_ref.shape[0]):
        total = total + parts_ref[j].astype(F32)
    for s in range(own_pairs):
        flux[s] = total[4 * s : 4 * s + 4, :]

    def fill(s, second):
        more = pair_forcing(s, left_ref, right_ref, picks, flux[s], force)
        forcing_ref[s] = pltpu.roll(more, 2 * PITCH - reach, 1)
        odd_ref[s] = (pair_rows(center_ref[2 * s], second, reach) + more).astype(BF)

    def fill_pair(s, carry):
        fill(s, center_ref[2 * s + 1])
        return carry

    def join(s, carry):
        even_ref[s] = jnp.concatenate([odd_ref[s][:, PITCH:], odd_ref[s + 1][:, :PITCH]], axis=1)
        return carry

    lax.fori_loop(0, own_pairs - 1, fill_pair, 0)
    fill(own_pairs - 1, center_ref[rows - 1])
    lax.fori_loop(0, own_pairs - 1, join, 0)
    even_ref[own_pairs - 1] = odd_ref[own_pairs - 1]
    for at, ref in ((0, first_ref), (rows - reach, last_ref)):
        for d in range(reach):
            half = (at + d) % 2
            ref[d] = odd_ref[(at + d) // 2][:, half * PITCH : (half + 1) * PITCH]


def wet_rows(center, left, right, picks, parts, force, reach):
    rows, ch, _ = center.shape
    edge = jax.ShapeDtypeStruct((reach, ch, PITCH), BF)
    pairs = (rows + 1) // 2
    own = jax.ShapeDtypeStruct((pairs, ch, 2 * PITCH), BF)
    return pl.pallas_call(
        functools.partial(wet_kernel, reach),
        out_shape=(own, own, jax.ShapeDtypeStruct(own.shape, F32), edge, edge),
        in_specs=[VMEM] * 6,
        out_specs=(VMEM,) * 5,
        scratch_shapes=[pltpu.VMEM((pairs, 4, 2 * PITCH), F32)],
        compiler_params=pltpu.CompilerParams(vmem_limit_bytes=24 << 20),
        cost_estimate=pl.CostEstimate(flops=1 << 20, bytes_accessed=1 << 20, transcendentals=0),
        name="wet_rows",
    )(center, left, right, picks, parts, force)


def ocean_kernel(
    reach, mask_tiles, center_ref, forcing_ref, odd_ref, even_ref, low_ref, high_ref, taps_ref, gain_ref,
    expand_ref, contract_ref, mask_ref, out_ref, odd, even, taps, gain, flag, smooth
):
    step = pl.program_id(0)
    _, ch, cols = center_ref.shape
    high_ch, wide = even.shape[1:]
    pairs = smooth.shape[0]
    side = 2 * reach + 1
    own_pairs = odd_ref.shape[0]

    @pl.when(step == 0)
    def _():
        def widen(s, carry):
            odd[s + 2, :ch, :] = odd_ref[s].astype(F32)
            even[s + 2, :ch, :] = even_ref[s].astype(F32)
            return carry

        lax.fori_loop(0, own_pairs, widen, 0)
        odd[0, :ch, PITCH:] = low_ref[0].astype(F32)
        odd[1, :ch, :] = jnp.concatenate([low_ref[1].astype(F32), low_ref[2].astype(F32)], axis=1)
        odd[own_pairs + 1, :ch, PITCH:] = high_ref[0].astype(F32)
        odd[own_pairs + 2, :ch, :] = jnp.concatenate(
            [high_ref[1].astype(F32), high_ref[2].astype(F32)], axis=1
        )
        for t in (0, 1, own_pairs + 1, own_pairs + 2):
            even[t] = jnp.concatenate([odd[t][:, PITCH:], odd[t + 1][:, :PITCH]], axis=1)
        for k in range(side * side):
            taps[k] = jnp.broadcast_to(taps_ref[:, k : k + 1], taps.shape[1:])
        gain[...] = jnp.broadcast_to(gain_ref[...], gain.shape)
        tall, across = mask_tiles
        mask = mask_ref[...].astype(F32).astype(BF)
        spread = 0.0
        for half in range(2):
            pair = lax.broadcasted_iota(jnp.int32, (32, 8), 0)
            tile = lax.broadcasted_iota(jnp.int32, (32, 8), 1)
            up = ((2 * pair + half) // tall == tile).astype(F32).astype(BF)
            lane = lax.broadcasted_iota(jnp.int32, (8, wide), 1) - half * PITCH
            tile = lax.broadcasted_iota(jnp.int32, (8, wide), 0)
            side_by = (lane >= 0) & (lane < cols) & (lane // across == tile)
            side_by = side_by.astype(F32).astype(BF)
            spread = spread + dot(dot(up, mask).astype(BF), side_by)
        for s in range(flag.shape[0]):
            flag[s] = jnp.broadcast_to(spread[s : s + 1, :], (8, wide))

    start = step * pairs

    def channels(c, carry):
        at = pl.multiple_of(c * 8, 8)
        total = [None] * pairs
        for dx in range(side):
            part = [None] * pairs
            for dy in range(side):
                tap = taps[dy * side + dx, pl.ds(at, 8), :]
                tap = jnp.concatenate([tap] * (wide // 128), axis=1)
                for p in range(pairs):
                    if dy % 2 == 0:
                        value = even[start + p + dy // 2, pl.ds(at, 8), :]
                    else:
                        value = odd[start + p + dy // 2 + 1, pl.ds(at, 8), :]
                    term = tap * value
                    part[p] = term if part[p] is None else part[p] + term
            for p in range(pairs):
                moved = part[p] if dx == 0 else pltpu.roll(part[p], wide - dx, 1)
                total[p] = moved if total[p] is None else total[p] + moved
        for p in range(pairs):
            smooth[p, pl.ds(at, 8), :] = total[p]
        return carry

    lax.fori_loop(0, high_ch // 8, channels, 0)
    scale = jnp.concatenate([gain[...]] * (wide // 128), axis=1)
    for p in range(pairs):
        value = smooth[p, :ch, :]
        value = value - jnp.mean(value, axis=0, keepdims=True)
        spread = jnp.mean(value * value, axis=0, keepdims=True)
        normed = (value * lax.rsqrt(spread + 1e-06) * scale).astype(BF)
        hidden = dot(expand_ref[...], normed)
        inner = hidden * (0.7978845608028654 + 0.035677408136300125 * (hidden * hidden))
        hidden = (hidden + hidden * jnp.tanh(inner)).astype(BF)
        branch = 0.5 * dot(contract_ref[...], hidden)
        change = flag[start + p][:1] * (forcing_ref[p] + branch)
        for half in range(2):
            moved = change[:, half * PITCH : half * PITCH + cols]
            out_ref[2 * p + half] = (center_ref[2 * p + half].astype(F32) + moved).astype(BF)


def ocean_block(
    center, forcing, odd, even, low, high, taps, gain, expand, contract, mask, mask_tiles, reach
):
    rows, ch, cols = center.shape
    pairs = 6
    steps = pl.cdiv((rows + 1) // 2, pairs)
    high_ch = pl.cdiv(ch, 8) * 8
    deep = steps * pairs + reach + 1
    whole = lambda a: pl.BlockSpec(a.shape, lambda g: (0,) * a.ndim)
    operands = (center, forcing, odd, even, low, high, taps, gain, expand, contract, mask)
    return pl.pallas_call(
        functools.partial(ocean_kernel, reach, mask_tiles),
        out_shape=jax.ShapeDtypeStruct(center.shape, BF),
        grid=(steps,),
        in_specs=[
            pl.BlockSpec((2 * pairs, ch, cols), lambda g: (g, 0, 0)),
            pl.BlockSpec((pairs, ch, 2 * PITCH), lambda g: (g, 0, 0)),
            *(whole(a) for a in operands[2:]),
        ],
        out_specs=pl.BlockSpec((2 * pairs, ch, cols), lambda g: (g, 0, 0)),
        scratch_shapes=[
            pltpu.VMEM((deep, high_ch, 2 * PITCH), F32),
            pltpu.VMEM((deep, high_ch, 2 * PITCH), F32),
            pltpu.VMEM((taps.shape[1], high_ch, 128), F32),
            pltpu.VMEM((ch, 128), F32),
            pltpu.VMEM((steps * pairs, 8, 2 * PITCH), F32),
            pltpu.VMEM((pairs, high_ch, 2 * PITCH), F32),
        ],
        compiler_params=pltpu.CompilerParams(vmem_limit_bytes=32 << 20),
        cost_estimate=pl.CostEstimate(
            flops=30 << 30, bytes_accessed=8 << 20, transcendentals=3 << 20
        ),
        name="ocean_block",
    )(*operands)


def shift(first, last, axis):
    count = lax.axis_size(axis)
    up = [(i, i + 1) for i in range(count - 1)]
    down = [(target, source) for source, target in up]
    return lax.ppermute(last, axis, up), lax.ppermute(first, axis, down)


def body(
    atmos,
    sea_temp_gain,
    legendre_analysis,
    legendre_synthesis,
    spectral_mixing_weight,
    surface_flux_weight,
    flux_ocean_forcing,
    ocean,
    ocean_tile_mask,
    depthwise_filter,
    norm_gain_vector,
    expand_matrix,
    contract_matrix,
):
    lat_parts = lax.axis_size("lat")
    chan_parts = lax.axis_size("chan")
    chan_at = lax.axis_index("chan")
    ch, rows, lon = atmos.shape
    per_dev, degrees, _ = legendre_analysis.shape
    ocean_ch, _, cols = ocean.shape
    reach = depthwise_filter.shape[2] // 2
    peers = lat_parts * chan_parts
    padded_rows = 2 * HALF

    table_fwd, table_inv = dft_tables(lon, peer_modes(lat_parts, chan_parts, per_dev))
    table_fwd, table_inv = jnp.asarray(table_fwd), jnp.asarray(table_inv)
    swap_out = jnp.asarray(row_swap(16, HALF))
    swap_in = jnp.asarray(row_swap(HALF, 16))

    x = jnp.transpose(atmos, (1, 0, 2))
    sea = jnp.transpose(ocean, (1, 0, 2))

    def exchange(wire):
        return lax.all_to_all(
            wire.reshape(peers, HALF, 8 * ch), ("chan", "lat"), 0, 0, tiled=True
        ).reshape(wire.shape)

    parts = flux_parts(x, sea, surface_flux_weight, reach, chan_parts)
    parts = lax.all_to_all(parts, "chan", 0, 0, tiled=True)

    gain = sea_temp_gain[None]
    at = jnp.reshape(chan_at * cols, (1,)).astype(jnp.int32)
    wire = forward(at, x, sea, gain, table_fwd, swap_out)
    gathered = exchange(wire)
    sea, legendre_analysis, legendre_synthesis, wire = lax.optimization_barrier(
        (sea, legendre_analysis, legendre_synthesis, wire)
    )
    left, right = shift(*edge_columns(sea, reach), "chan")
    force = flux_ocean_forcing.T
    force_high = force.astype(BF)
    force_low = (force - force_high.astype(F32)).astype(BF)
    force = jnp.concatenate([force_high, force_high, force_low, jnp.zeros_like(force_low)], axis=0)
    picks = jnp.asarray(edge_picks(reach, cols + 2 * reach))
    odd, even, forcing, first, last = wet_rows(sea, left, right, picks, parts, force, reach)
    low, high = shift(first, last, "lat")

    def banded(table):
        table = table.reshape(per_dev, lat_parts, rows, degrees)
        table = jnp.pad(table, ((0, 0), (0, 0), (0, padded_rows - rows), (0, 0)))
        table = table.reshape(per_dev, lat_parts, HALF, 2, degrees).transpose(0, 3, 1, 2, 4)
        return table.reshape(per_dev, 2, lat_parts * HALF, degrees)

    analysis = banded(jnp.transpose(legendre_analysis, (0, 2, 1)))
    synthesis = banded(legendre_synthesis)
    analysis, first, last = lax.optimization_barrier((analysis, first, last))
    back = spectral(
        gathered, analysis, synthesis, spectral_mixing_weight, jnp.asarray(spread_last(lat_parts))
    )
    back, low, high = lax.optimization_barrier((back, low, high))
    returned = exchange(back)

    tile_rows, tile_cols = ocean_tile_mask.shape
    mask = jnp.pad(ocean_tile_mask, ((0, 8 - tile_rows), (0, 8 - tile_cols)))
    taps = depthwise_filter.reshape(ocean_ch, -1).astype(F32)
    taps = jnp.pad(taps, ((0, -ocean_ch % 8), (0, 0)))
    ocean_next = ocean_block(
        sea,
        forcing,
        odd,
        even,
        low,
        high,
        taps,
        norm_gain_vector[:, None],
        expand_matrix,
        contract_matrix,
        mask,
        (rows // tile_rows, cols // tile_cols),
        reach,
    )

    atmos_next = inverse(returned, table_inv, swap_in, x, gain, parts)
    return (jnp.transpose(atmos_next, (1, 0, 2)), jnp.transpose(ocean_next, (1, 0, 2)))


def solution(mesh):
    in_specs = (
        P("chan", "lat", None),
        P("chan"),
        P(("lat", "chan"), None, None),
        P(("lat", "chan"), None, None),
        P(),
        P(None, "chan"),
        P(),
        P(None, "lat", "chan"),
        P("lat", "chan"),
        P(),
        P(),
        P(),
        P(),
    )
    out_specs = (P("chan", "lat", None), P(None, "lat", "chan"))
    return jax.shard_map(body, mesh=mesh, in_specs=in_specs, out_specs=out_specs, check_vma=False)
```

```python
import functools
import math

import jax
import jax.numpy as jnp
import ml_dtypes
import numpy as np
from jax import lax
from jax.experimental import pallas as pl
from jax.experimental.pallas import tpu as pltpu
from jax.sharding import PartitionSpec as P

BF = jnp.bfloat16
F32 = jnp.float32
VMEM = pl.BlockSpec(memory_space=pltpu.VMEM)
NT = (((1,), (1,)), ((), ()))

HALF = 24


def peer_modes(lat_parts, chan_parts, per_dev):
    j, i, mm = np.meshgrid(np.arange(chan_parts), np.arange(lat_parts), np.arange(per_dev), indexing="ij")
    return ((i * chan_parts + j) * per_dev + mm).reshape(lat_parts * chan_parts, per_dev)


def dft_tables(lon_len, modes):
    total = modes.size
    product = np.arange(lon_len)[:, None, None] * modes.T[None]
    angle = np.float32(2.0 * math.pi / lon_len) * (product % lon_len).astype(np.float32)
    cos, sin = np.cos(angle), np.sin(angle)
    factor = np.float32(math.sqrt(2.0 / lon_len))
    forward = np.stack([factor * cos, -factor * sin], axis=2).reshape(lon_len, total * 2)
    back = np.float32(1.0 / math.sqrt(total))
    inverse = np.stack([back * cos, -back * sin], axis=2).reshape(lon_len, total * 2).T
    return forward.astype(ml_dtypes.bfloat16), np.ascontiguousarray(inverse).astype(ml_dtypes.bfloat16)


def row_swap(outer, inner):
    n = outer * inner
    swap = np.zeros((n, n), np.float32)
    o, k = np.meshgrid(np.arange(outer), np.arange(inner), indexing="ij")
    swap[(o * inner + k).ravel(), (k * outer + o).ravel()] = 1.0
    return swap.astype(ml_dtypes.bfloat16)


def dot(a, b, dims=(((1,), (0,)), ((), ()))):
    return lax.dot_general(a, b, dims, preferred_element_type=F32)


ANY = pl.BlockSpec(memory_space=pl.ANY)
SMEM = pl.BlockSpec(memory_space=pltpu.SMEM)
HBM = pl.BlockSpec(memory_space=pltpu.HBM)
BLOCK = 6


def row_groups(rows):
    return [(at, min(BLOCK, rows - at)) for at in range(0, rows, BLOCK)]


def column(row_ref):
    n = row_ref.shape[1]
    rows = jnp.broadcast_to(row_ref[...].astype(F32), (16, n))
    first = lax.broadcasted_iota(jnp.int32, (16, 128), 0) == 0
    return dot(rows.astype(BF), first.astype(F32).astype(BF), (((0,), (0,)), ((), ())))


def pieces_of(rows):
    return [(0, BLOCK), (BLOCK, 3 * BLOCK), (4 * BLOCK, rows - 4 * BLOCK)]


def copy_pieces(source, target, pieces, sems):
    copies = {}
    for k, (at, size) in enumerate(pieces):
        span = pl.ds(at, size)
        copies[at] = pltpu.make_async_copy(source.at[span], target.at[span], sems.at[k])
        copies[at].start()
    return copies


def forward_kernel(
    at_ref, x_ref, sea_ref, gain_ref, table_ref, swap_ref, out_ref,
    x, sea, table, held, out, x_sems, out_sems, sems
):
    rows, ch, lon = x.shape
    peers = held.shape[1]
    groups = row_groups(rows)
    table_copy = pltpu.make_async_copy(table_ref, table, sems.at[1])
    table_copy.start()
    x_copies = copy_pieces(x_ref, x, pieces_of(rows), x_sems)
    sea_copy = pltpu.make_async_copy(sea_ref.at[:, pl.ds(0, 16), :], sea, sems.at[0])
    sea_copy.start()
    table_copy.wait()
    for at, size in groups:
        if at in x_copies:
            x_copies[at].wait()
        y = dot(x[at : at + size].reshape(size * ch, lon), table[...]).astype(BF)
        for a in range(0, size, 2):
            pieces = []
            for rh in range(2):
                for q in range(4):
                    if a + rh < size:
                        pieces.append(y[(a + rh) * ch : (a + rh + 1) * ch, q * peers : (q + 1) * peers])
                    else:
                        pieces.append(jnp.zeros((ch, peers), BF))
            held[(at + a) // 2] = jnp.concatenate(pieces, axis=0).T

    sea_copy.wait()
    own = sea[:, 0, :].astype(F32)
    own = jnp.concatenate([own, jnp.zeros((ch - rows, own.shape[1]), F32)], axis=0)
    wide = pl.cdiv(lon, 128) * 128
    own = jnp.concatenate([own, jnp.zeros((ch, wide - own.shape[1]), F32)], axis=1)
    own = pltpu.roll(own, at_ref[0] * sea.shape[2], 1)[:, :lon].astype(BF)
    y = dot(own, table[...]).astype(BF)
    pieces = [y[:, q * peers : (q + 1) * peers] for q in range(4)]
    pieces.append(column(gain_ref).astype(BF))
    pieces.append(jnp.zeros((3 * ch, peers), BF))
    held[HALF - 1] = jnp.concatenate(pieces, axis=0).T

    out_copies = []
    half = peers * HALF // 2
    for b in range(peers // 16):
        part = held[:, b * 16 : (b + 1) * 16, :].reshape(HALF * 16, held.shape[2])
        span = pl.ds(b * 16 * HALF, 16 * HALF)
        out[span, :] = dot(swap_ref[...], part).astype(BF)
        if (b + 1) * 16 * HALF % half == 0:
            k = len(out_copies)
            span = pl.ds(k * half, half)
            out_copies.append(pltpu.make_async_copy(out.at[span], out_ref.at[span], out_sems.at[k]))
            out_copies[-1].start()
    for copy in out_copies:
        copy.wait()


def forward(at, x, sea, gain, table, swap):
    rows, ch, lon = x.shape
    peers = table.shape[1] // 4
    return pl.pallas_call(
        forward_kernel,
        out_shape=pltpu.HBM((peers * HALF, 8 * ch), BF),
        in_specs=[SMEM, ANY, ANY, VMEM, ANY, VMEM],
        out_specs=ANY,
        scratch_shapes=[
            pltpu.VMEM(x.shape, BF),
            pltpu.VMEM((rows, 16, sea.shape[2]), BF),
            pltpu.VMEM(table.shape, BF),
            pltpu.VMEM((HALF, peers, 8 * ch), BF),
            pltpu.VMEM((peers * HALF, 8 * ch), BF),
            pltpu.SemaphoreType.DMA((3,)),
            pltpu.SemaphoreType.DMA((2,)),
            pltpu.SemaphoreType.DMA((2,)),
        ],
        compiler_params=pltpu.CompilerParams(vmem_limit_bytes=58 << 20),
        cost_estimate=pl.CostEstimate(
            flops=2 * rows * ch * lon * peers * 4, bytes_accessed=14 << 20, transcendentals=0
        ),
        name="dft_forward",
    )(at, x, sea, gain, table, swap)


def spread_last(lat_parts):
    n = lat_parts * HALF
    col = np.arange(n)
    spread = np.zeros((n, n), np.float32)
    spread[col // HALF * HALF + HALF - 1, col] = 1.0
    return spread.astype(ml_dtypes.bfloat16)


def spectral_kernel(
    wire_hbm, analysis_hbm, synthesis_hbm, mix_hbm, spread_hbm, out_ref,
    wire_ref, analysis_ref, synthesis_ref, mix_ref, spread_ref, spec, mixed, gains, out,
    wire_sems, in_sems, sems
):
    size = analysis_ref.shape[2]
    ch = wire_ref.shape[1] // 8
    groups = wire_ref.shape[0] // size
    pairs = (
        (analysis_hbm, analysis_ref), (spread_hbm, spread_ref), (mix_hbm, mix_ref), (synthesis_hbm, synthesis_ref)
    )
    tables = [pltpu.make_async_copy(a, b, in_sems.at[k]) for k, (a, b) in enumerate(pairs)]
    tables[0].start()
    wires = copy_pieces(wire_hbm, wire_ref, [(0, 2 * size), (2 * size, (groups - 2) * size)], wire_sems)
    for copy in tables[1:]:
        copy.start()
    tables[0].wait()
    lines = 0.0
    for j in range(groups):
        if j * size in wires:
            wires[j * size].wait()
        turned = wire_ref[j * size : (j + 1) * size, :].T
        for m in range(2):
            total = sum(
                dot(turned[(4 * rh + 2 * m) * ch : (4 * rh + 2 * m + 2) * ch, :], analysis_ref[m, rh])
                for rh in range(2)
            ).astype(BF)
            for k in range(2):
                spec[m, k, j * ch : (j + 1) * ch, :] = total[k * ch : (k + 1) * ch, :]
        gains[j * ch : (j + 1) * ch, :] = turned[4 * ch : 5 * ch, :128]
        lines = lines + turned[: 4 * ch, :].astype(F32)

    for copy in tables[1:]:
        copy.wait()
    lines = dot(lines.astype(BF), spread_ref[...])
    own_row = lax.broadcasted_iota(jnp.int32, (ch, size), 0)
    rr = lax.rem(lax.broadcasted_iota(jnp.int32, (ch, size), 1), HALF)
    real, imag = mix_ref[0], mix_ref[1]
    gain_real = dot(real, gains[...])[:, HALF - 1 : HALF]
    gain_imag = dot(imag, gains[...])[:, HALF - 1 : HALF]
    for m in range(2):
        surface = 0.0
        for rh in range(2):
            both = [
                jnp.sum(
                    jnp.where(own_row == 2 * rr + rh, lines[q * ch : (q + 1) * ch, :], 0.0),
                    axis=0,
                    keepdims=True,
                )
                for q in (2 * m, 2 * m + 1)
            ]
            both.append(jnp.zeros((6, size), F32))
            both = jnp.concatenate(both, axis=0).astype(BF)
            surface = surface + dot(both, analysis_ref[m, rh])
        sr, si = surface[0:1, :], surface[1:2, :]
        value = dot(real, spec[m, 0]) - dot(imag, spec[m, 1])
        mixed[m, 0] = (value + (gain_real * sr - gain_imag * si)).astype(BF)
        value = dot(imag, spec[m, 0]) + dot(real, spec[m, 1])
        mixed[m, 1] = (value + (gain_imag * sr + gain_real * si)).astype(BF)

    copies = []
    for j in range(groups):
        pieces = []
        for rh in range(2):
            for m in range(2):
                both = [mixed[m, k, j * ch : (j + 1) * ch, :] for k in range(2)]
                pieces.append(dot(synthesis_ref[m, rh], jnp.concatenate(both, axis=0), NT).astype(BF))
        out[j * size : (j + 1) * size, :] = jnp.concatenate(pieces, axis=1)
        if j % 4 == 3:
            span = pl.ds((j - 3) * size, 4 * size)
            copies.append(pltpu.make_async_copy(out.at[span], out_ref.at[span], sems.at[j // 4]))
            copies[-1].start()
    for copy in copies:
        copy.wait()


def spectral(wire, analysis, synthesis, mix, spread):
    _, _, size, degrees = analysis.shape
    groups = wire.shape[0] // size
    all_ch = mix.shape[1]
    return pl.pallas_call(
        spectral_kernel,
        out_shape=pltpu.HBM(wire.shape, BF),
        in_specs=[ANY] * 5,
        out_specs=ANY,
        scratch_shapes=[
            *(pltpu.VMEM(a.shape, BF) for a in (wire, analysis, synthesis, mix, spread)),
            pltpu.VMEM((2, 2, all_ch, degrees), BF),
            pltpu.VMEM((2, 2, all_ch, degrees), BF),
            pltpu.VMEM((all_ch, 128), BF),
            pltpu.VMEM(wire.shape, BF),
            pltpu.SemaphoreType.DMA((groups,)),
            pltpu.SemaphoreType.DMA((4,)),
            pltpu.SemaphoreType.DMA((groups,)),
        ],
        compiler_params=pltpu.CompilerParams(vmem_limit_bytes=56 << 20),
        cost_estimate=pl.CostEstimate(flops=2 << 30, bytes_accessed=9 << 20, transcendentals=0),
        name="spectral",
    )(wire, analysis, synthesis, mix, spread)


def inverse_kernel(
    wire_ref, table_ref, swap_ref, x_ref, gain_ref, parts_ref, out_ref,
    wire, table, held, x, out, lines, wire_sems, x_sems, out_sems, sems
):
    rows, ch, lon = x.shape
    peers = held.shape[1]
    groups = row_groups(rows)
    turn = 16 * HALF
    wires = copy_pieces(wire_ref, wire, [(0, 2 * turn), (2 * turn, peers * HALF - 2 * turn)], wire_sems)
    table_copy = pltpu.make_async_copy(table_ref, table, sems.at[0])
    table_copy.start()
    x_copies = copy_pieces(x_ref, x, pieces_of(rows), x_sems)
    for b in range(peers // 16):
        if b * turn in wires:
            wires[b * turn].wait()
        part = dot(swap_ref[...], wire[b * turn : (b + 1) * turn, :]).astype(BF)
        held[:, b * 16 : (b + 1) * 16, :] = part.reshape(HALF, 16, held.shape[2])
    chans = parts_ref.shape[0]
    for half in range(2):
        lines[half] = jnp.concatenate(
            [
                parts_ref[j, SURFACE:EDGES, half * PITCH : half * PITCH + lon // chans].astype(F32)
                for j in range(chans)
            ],
            axis=1,
        )
    gain = column(gain_ref)[:, :1]
    table_copy.wait()

    def wave_of(at, size):
        waves = []
        for a in range(0, size, 2):
            turned = held[(at + a) // 2].T
            for rh in range(min(2, size - a)):
                parts = [turned[(4 * rh + q) * ch : (4 * rh + q + 1) * ch, :] for q in range(4)]
                waves.append(jnp.concatenate(parts, axis=1))
        return dot(jnp.concatenate(waves, axis=0), table[...])

    out_copies = []
    wave = wave_of(*groups[0])
    for g, (at, size) in enumerate(groups):
        if at in x_copies:
            x_copies[at].wait()
        later = wave_of(*groups[g + 1]) if g + 1 < len(groups) else None
        for a in range(size):
            line = lines[a % 2, (at + a) // 2 : (at + a) // 2 + 1, :]
            forced = x[at + a].astype(F32) + gain * line
            out[at + a] = (forced + wave[a * ch : (a + 1) * ch, :]).astype(BF)
        if g % 2 or g + 1 == len(groups):
            span = pl.ds(BLOCK * (g - g % 2), at + size - BLOCK * (g - g % 2))
            out_copies.append(pltpu.make_async_copy(out.at[span], out_ref.at[span], out_sems.at[g]))
            out_copies[-1].start()
        wave = later
    for copy in out_copies:
        copy.wait()


def inverse(wire, table, swap, x, gain, parts):
    rows, ch, lon = x.shape
    peers = table.shape[0] // 4
    groups = len(row_groups(rows))
    return pl.pallas_call(
        inverse_kernel,
        out_shape=pltpu.HBM(x.shape, BF),
        in_specs=[ANY, ANY, VMEM, ANY, VMEM, VMEM],
        out_specs=ANY,
        scratch_shapes=[
            pltpu.VMEM(wire.shape, BF),
            pltpu.VMEM(table.shape, BF),
            pltpu.VMEM((HALF, peers, 8 * ch), BF),
            pltpu.VMEM(x.shape, BF),
            pltpu.VMEM(x.shape, BF),
            pltpu.VMEM((2, HALF, lon), F32),
            pltpu.SemaphoreType.DMA((peers // 16,)),
            pltpu.SemaphoreType.DMA((groups,)),
            pltpu.SemaphoreType.DMA((groups,)),
            pltpu.SemaphoreType.DMA((1,)),
        ],
        compiler_params=pltpu.CompilerParams(vmem_limit_bytes=56 << 20),
        cost_estimate=pl.CostEstimate(
            flops=2 * rows * ch * lon * peers * 4, bytes_accessed=20 << 20, transcendentals=0
        ),
        name="dft_inverse",
    )(wire, table, swap, x, gain, parts)


PITCH = 192


SURFACE = 4 * HALF
EDGES = SURFACE + HALF
PILE = 5


def flux_kernel(reach, at_ref, x_ref, sea_ref, weight_ref, out_ref, x, sea, x_sems, sems):
    rows, ch, lon = x.shape
    _, oc, cols = sea.shape
    peers = out_ref.shape[0]
    tile = lon // peers
    block = 8
    x_copies = {}
    for k, (at, size) in enumerate([(0, 2 * block), (2 * block, 2 * block), (4 * block, rows - 4 * block)]):
        span = pl.ds(at, size)
        x_copies[at] = pltpu.make_async_copy(x_ref.at[span], x.at[span], x_sems.at[k])
    sea_copy = pltpu.make_async_copy(sea_ref, sea, sems.at[0])
    sea_copy.start()
    for copy in x_copies.values():
        copy.start()

    sea_copy.wait()
    own = jnp.concatenate([sea[:, 0, :].astype(F32), jnp.zeros((ch - rows, tile), F32)], axis=0)
    halves = []
    for half in range(2):
        pick = lax.broadcasted_iota(jnp.int32, (HALF, ch), 1) == (
            2 * lax.broadcasted_iota(jnp.int32, (HALF, ch), 0) + half
        )
        halves.append(dot(pick.astype(F32).astype(BF), own.astype(BF)))
        halves.append(jnp.zeros((HALF, PITCH - tile), F32))
    own = jnp.concatenate(halves, axis=1)

    row = lax.broadcasted_iota(jnp.int32, (16, cols), 0)
    col = lax.broadcasted_iota(jnp.int32, (16, cols), 1)
    want = jnp.where(row % 8 < 2 * reach, row % 8 % reach + row // 8 * (cols - reach), -1)
    picks = [
        ((col == want) & (row % 8 // reach == half)).astype(F32).astype(BF) for half in range(2)
    ]
    piles = [[], []]
    for s in range(pl.cdiv(rows, 2)):
        value = dot(picks[0], sea[2 * s], NT)
        if 2 * s + 1 < rows:
            value = value + dot(picks[1], sea[2 * s + 1], NT)
        piles[0].append(value[:8])
        piles[1].append(value[8:])
    edges = []
    for pile in piles:
        pile = pile + [jnp.zeros((8, oc), F32)] * (-len(pile) % PILE)
        wide = [jnp.concatenate(pile[k : k + PILE], axis=0) for k in range(0, len(pile), PILE)]
        wide.append(jnp.zeros((8 * PILE, 2 * PITCH - oc * len(wide)), F32))
        edges.append(jnp.concatenate(wide, axis=1))
    no_edge = jnp.zeros_like(edges[0])
    for j in range(peers):
        edge = jnp.where(at_ref[0] == j + 1, edges[0], jnp.where(at_ref[0] == j - 1, edges[1], no_edge))
        out_ref[j, SURFACE:, :] = jnp.concatenate([own, edge], axis=0).astype(BF)

    weight = weight_ref[...].astype(F32)
    weight = jnp.concatenate([weight] * block, axis=1)
    weight = jnp.concatenate([weight] * block, axis=0)
    row = lax.broadcasted_iota(jnp.int32, weight.shape, 0)
    col = lax.broadcasted_iota(jnp.int32, weight.shape, 1)
    keep = col // ch == row % 16 // 4 * 2 + row // 16
    weight = jnp.where(keep, weight, 0.0).astype(BF)
    before = jnp.zeros((4 * block, reach), F32)
    after = jnp.zeros((4 * block, PITCH - tile - reach), F32)
    for g, at in enumerate(range(0, rows, block)):
        size = min(block, rows - at)
        if at in x_copies:
            x_copies[at].wait()
        y = dot(weight[:, : size * ch], x[at : at + size].reshape(size * ch, lon))
        y = jnp.concatenate([before, y, after], axis=1)
        for j in range(peers):
            part = y[:, tile * j : tile * j + PITCH]
            part = jnp.concatenate([part[: 2 * block], part[2 * block :]], axis=1)
            out_ref[j, 2 * block * g : 2 * block * (g + 1), :] = part.astype(BF)


def flux_parts(at, x, sea, weight, reach, peers):
    return pl.pallas_call(
        functools.partial(flux_kernel, reach),
        out_shape=jax.ShapeDtypeStruct((peers, EDGES + 8 * PILE, 2 * PITCH), BF),
        in_specs=[SMEM, ANY, ANY, VMEM],
        out_specs=VMEM,
        scratch_shapes=[
            pltpu.VMEM(x.shape, BF),
            pltpu.VMEM(sea.shape, BF),
            pltpu.SemaphoreType.DMA((3,)),
            pltpu.SemaphoreType.DMA((1,)),
        ],
        compiler_params=pltpu.CompilerParams(vmem_limit_bytes=58 << 20),
        cost_estimate=pl.CostEstimate(flops=1 << 30, bytes_accessed=7 << 20, transcendentals=0),
        name="flux_parts",
    )(at, x, sea, weight)


def edge_picks(reach, span):
    picks = np.zeros((16, 2 * PITCH), np.float32)
    for side in range(2):
        for half in range(2):
            for dx in range(reach):
                picks[8 * side + reach * half + dx, PITCH * half + side * (span - reach) + dx] = 1.0
    return picks.astype(ml_dtypes.bfloat16)


def pair_forcing(s, left_ref, right_ref, picks, flux, force):
    high = flux.astype(BF).astype(F32)
    low = flux - high
    flux = jnp.concatenate([high, low, high, jnp.zeros_like(high)], axis=0).astype(BF)
    edge = jnp.concatenate([left_ref[s], right_ref[s]], axis=0).astype(BF)
    return dot(
        jnp.concatenate([edge, force], axis=0),
        jnp.concatenate([picks, flux], axis=0),
        (((0,), (0,)), ((), ())),
    )


def pair_rows(first, second, reach):
    ch, cols = first.shape
    before = jnp.zeros((ch, reach), F32)
    after = jnp.zeros((ch, PITCH - cols - reach), F32)
    first, second = first.astype(F32), second.astype(F32)
    return jnp.concatenate([before, first, after, before, second, after], axis=1)


def wet_kernel(
    reach, at_ref, center_ref, picks_ref, parts_ref, force_ref,
    odd_ref, even_ref, forcing_ref, first_ref, last_ref, flux, left_ref, right_ref
):
    rows, ch, _ = center_ref.shape
    own_pairs = odd_ref.shape[0]
    peers = parts_ref.shape[0]
    picks, force = picks_ref[...], force_ref[...]
    total = parts_ref[0, :SURFACE, :].astype(F32)
    for j in range(1, peers):
        total = total + parts_ref[j, :SURFACE, :].astype(F32)
    at = at_ref[0]
    left = parts_ref[jnp.maximum(at - 1, 0), EDGES:, :].astype(F32)
    right = parts_ref[jnp.minimum(at + 1, peers - 1), EDGES:, :].astype(F32)
    for s in range(own_pairs):
        flux[s] = total[4 * s : 4 * s + 4, :]
        span, lanes = slice(8 * (s % PILE), 8 * (s % PILE) + 8), slice(ch * (s // PILE), ch * (s // PILE) + ch)
        left_ref[s] = left[span, lanes]
        right_ref[s] = right[span, lanes]

    def fill(s, second):
        more = pair_forcing(s, left_ref, right_ref, picks, flux[s], force)
        forcing_ref[s] = pltpu.roll(more, 2 * PITCH - reach, 1)
        odd_ref[s] = (pair_rows(center_ref[2 * s], second, reach) + more).astype(BF)

    def fill_pair(s, carry):
        fill(s, center_ref[2 * s + 1])
        return carry

    def join(s, carry):
        even_ref[s] = jnp.concatenate([odd_ref[s][:, PITCH:], odd_ref[s + 1][:, :PITCH]], axis=1)
        return carry

    lax.fori_loop(0, own_pairs - 1, fill_pair, 0)
    fill(own_pairs - 1, center_ref[rows - 1])
    lax.fori_loop(0, own_pairs - 1, join, 0)
    even_ref[own_pairs - 1] = odd_ref[own_pairs - 1]
    for at, ref in ((0, first_ref), (rows - reach, last_ref)):
        for d in range(reach):
            half = (at + d) % 2
            ref[d] = odd_ref[(at + d) // 2][:, half * PITCH : (half + 1) * PITCH]


def wet_rows(at, center, picks, parts, force, reach):
    rows, ch, _ = center.shape
    edge = jax.ShapeDtypeStruct((reach, ch, PITCH), BF)
    pairs = (rows + 1) // 2
    own = jax.ShapeDtypeStruct((pairs, ch, 2 * PITCH), BF)
    return pl.pallas_call(
        functools.partial(wet_kernel, reach),
        out_shape=(own, own, jax.ShapeDtypeStruct(own.shape, F32), edge, edge),
        in_specs=[SMEM] + [VMEM] * 4,
        out_specs=(VMEM,) * 5,
        scratch_shapes=[
            pltpu.VMEM((pairs, 4, 2 * PITCH), F32),
            pltpu.VMEM((pairs, 8, ch), F32),
            pltpu.VMEM((pairs, 8, ch), F32),
        ],
        compiler_params=pltpu.CompilerParams(vmem_limit_bytes=24 << 20),
        cost_estimate=pl.CostEstimate(flops=1 << 20, bytes_accessed=1 << 20, transcendentals=0),
        name="wet_rows",
    )(at, center, picks, parts, force)


def ocean_kernel(
    reach, mask_tiles, center_ref, forcing_ref, odd_ref, even_ref, low_ref, high_ref, taps_ref, gain_ref,
    expand_ref, contract_ref, mask_ref, out_ref, odd, even, taps, gain, flag, smooth
):
    step = pl.program_id(0)
    _, ch, cols = center_ref.shape
    high_ch, wide = even.shape[1:]
    pairs = smooth.shape[0]
    side = 2 * reach + 1
    own_pairs = odd_ref.shape[0]

    @pl.when(step == 0)
    def _():
        def widen(s, carry):
            odd[s + 2, :ch, :] = odd_ref[s].astype(F32)
            even[s + 2, :ch, :] = even_ref[s].astype(F32)
            return carry

        lax.fori_loop(0, own_pairs, widen, 0)
        odd[0, :ch, PITCH:] = low_ref[0].astype(F32)
        odd[1, :ch, :] = jnp.concatenate([low_ref[1].astype(F32), low_ref[2].astype(F32)], axis=1)
        odd[own_pairs + 1, :ch, PITCH:] = high_ref[0].astype(F32)
        odd[own_pairs + 2, :ch, :] = jnp.concatenate(
            [high_ref[1].astype(F32), high_ref[2].astype(F32)], axis=1
        )
        for t in (0, 1, own_pairs + 1, own_pairs + 2):
            even[t] = jnp.concatenate([odd[t][:, PITCH:], odd[t + 1][:, :PITCH]], axis=1)
        for k in range(side * side):
            taps[k] = jnp.broadcast_to(taps_ref[:, k : k + 1], taps.shape[1:])
        gain[...] = jnp.broadcast_to(gain_ref[...], gain.shape)
        tall, across = mask_tiles
        mask = mask_ref[...].astype(F32).astype(BF)
        spread = 0.0
        for half in range(2):
            pair = lax.broadcasted_iota(jnp.int32, (32, 8), 0)
            tile = lax.broadcasted_iota(jnp.int32, (32, 8), 1)
            up = ((2 * pair + half) // tall == tile).astype(F32).astype(BF)
            lane = lax.broadcasted_iota(jnp.int32, (8, wide), 1) - half * PITCH
            tile = lax.broadcasted_iota(jnp.int32, (8, wide), 0)
            side_by = (lane >= 0) & (lane < cols) & (lane // across == tile)
            side_by = side_by.astype(F32).astype(BF)
            spread = spread + dot(dot(up, mask).astype(BF), side_by)
        for s in range(flag.shape[0]):
            flag[s] = jnp.broadcast_to(spread[s : s + 1, :], (8, wide))

    start = step * pairs

    def channels(c, carry):
        at = pl.multiple_of(c * 8, 8)
        total = [None] * pairs
        for dx in range(side):
            part = [None] * pairs
            for dy in range(side):
                tap = taps[dy * side + dx, pl.ds(at, 8), :]
                tap = jnp.concatenate([tap] * (wide // 128), axis=1)
                for p in range(pairs):
                    if dy % 2 == 0:
                        value = even[start + p + dy // 2, pl.ds(at, 8), :]
                    else:
                        value = odd[start + p + dy // 2 + 1, pl.ds(at, 8), :]
                    term = tap * value
                    part[p] = term if part[p] is None else part[p] + term
            for p in range(pairs):
                moved = part[p] if dx == 0 else pltpu.roll(part[p], wide - dx, 1)
                total[p] = moved if total[p] is None else total[p] + moved
        for p in range(pairs):
            smooth[p, pl.ds(at, 8), :] = total[p]
        return carry

    lax.fori_loop(0, high_ch // 8, channels, 0)
    scale = jnp.concatenate([gain[...]] * (wide // 128), axis=1)
    for p in range(pairs):
        value = smooth[p, :ch, :]
        value = value - jnp.mean(value, axis=0, keepdims=True)
        spread = jnp.mean(value * value, axis=0, keepdims=True)
        normed = (value * lax.rsqrt(spread + 1e-06) * scale).astype(BF)
        hidden = dot(expand_ref[...], normed)
        inner = hidden * (0.7978845608028654 + 0.035677408136300125 * (hidden * hidden))
        hidden = (hidden + hidden * jnp.tanh(inner)).astype(BF)
        branch = 0.5 * dot(contract_ref[...], hidden)
        change = flag[start + p][:1] * (forcing_ref[p] + branch)
        for half in range(2):
            moved = change[:, half * PITCH : half * PITCH + cols]
            out_ref[2 * p + half] = (center_ref[2 * p + half].astype(F32) + moved).astype(BF)


def ocean_block(
    center, forcing, odd, even, low, high, taps, gain, expand, contract, mask, mask_tiles, reach
):
    rows, ch, cols = center.shape
    pairs = 6
    steps = pl.cdiv((rows + 1) // 2, pairs)
    high_ch = pl.cdiv(ch, 8) * 8
    deep = steps * pairs + reach + 1
    whole = lambda a: pl.BlockSpec(a.shape, lambda g: (0,) * a.ndim)
    operands = (center, forcing, odd, even, low, high, taps, gain, expand, contract, mask)
    return pl.pallas_call(
        functools.partial(ocean_kernel, reach, mask_tiles),
        out_shape=jax.ShapeDtypeStruct(center.shape, BF),
        grid=(steps,),
        in_specs=[
            pl.BlockSpec((2 * pairs, ch, cols), lambda g: (g, 0, 0)),
            pl.BlockSpec((pairs, ch, 2 * PITCH), lambda g: (g, 0, 0)),
            *(whole(a) for a in operands[2:]),
        ],
        out_specs=pl.BlockSpec((2 * pairs, ch, cols), lambda g: (g, 0, 0)),
        scratch_shapes=[
            pltpu.VMEM((deep, high_ch, 2 * PITCH), F32),
            pltpu.VMEM((deep, high_ch, 2 * PITCH), F32),
            pltpu.VMEM((taps.shape[1], high_ch, 128), F32),
            pltpu.VMEM((ch, 128), F32),
            pltpu.VMEM((steps * pairs, 8, 2 * PITCH), F32),
            pltpu.VMEM((pairs, high_ch, 2 * PITCH), F32),
        ],
        compiler_params=pltpu.CompilerParams(vmem_limit_bytes=32 << 20),
        cost_estimate=pl.CostEstimate(
            flops=30 << 30, bytes_accessed=8 << 20, transcendentals=3 << 20
        ),
        name="ocean_block",
    )(*operands)


def shift(first, last, axis):
    count = lax.axis_size(axis)
    up = [(i, i + 1) for i in range(count - 1)]
    down = [(target, source) for source, target in up]
    return lax.ppermute(last, axis, up), lax.ppermute(first, axis, down)


def body(
    atmos,
    sea_temp_gain,
    legendre_analysis,
    legendre_synthesis,
    spectral_mixing_weight,
    surface_flux_weight,
    flux_ocean_forcing,
    ocean,
    ocean_tile_mask,
    depthwise_filter,
    norm_gain_vector,
    expand_matrix,
    contract_matrix,
):
    lat_parts = lax.axis_size("lat")
    chan_parts = lax.axis_size("chan")
    chan_at = lax.axis_index("chan")
    ch, rows, lon = atmos.shape
    per_dev, degrees, _ = legendre_analysis.shape
    ocean_ch, _, cols = ocean.shape
    reach = depthwise_filter.shape[2] // 2
    peers = lat_parts * chan_parts
    padded_rows = 2 * HALF

    table_fwd, table_inv = dft_tables(lon, peer_modes(lat_parts, chan_parts, per_dev))
    table_fwd, table_inv = jnp.asarray(table_fwd), jnp.asarray(table_inv)
    swap_out = jnp.asarray(row_swap(16, HALF))
    swap_in = jnp.asarray(row_swap(HALF, 16))

    x = jnp.transpose(atmos, (1, 0, 2))
    sea = jnp.transpose(ocean, (1, 0, 2))

    def exchange(wire):
        return lax.all_to_all(
            wire.reshape(peers, HALF, 8 * ch), ("chan", "lat"), 0, 0, tiled=True
        ).reshape(wire.shape)

    at = jnp.reshape(chan_at, (1,)).astype(jnp.int32)
    parts = flux_parts(at, x, sea, surface_flux_weight, reach, chan_parts)
    parts = lax.all_to_all(parts, "chan", 0, 0, tiled=True)

    gain = sea_temp_gain[None]
    wire = forward(at, x, sea, gain, table_fwd, swap_out)
    gathered = exchange(wire)
    sea, legendre_analysis, legendre_synthesis, wire = lax.optimization_barrier(
        (sea, legendre_analysis, legendre_synthesis, wire)
    )
    force = flux_ocean_forcing.T
    force_high = force.astype(BF)
    force_low = (force - force_high.astype(F32)).astype(BF)
    force = jnp.concatenate([force_high, force_high, force_low, jnp.zeros_like(force_low)], axis=0)
    picks = jnp.asarray(edge_picks(reach, cols + 2 * reach))
    odd, even, forcing, first, last = wet_rows(at, sea, picks, parts, force, reach)
    low, high = shift(first, last, "lat")

    def banded(table):
        table = table.reshape(per_dev, lat_parts, rows, degrees)
        table = jnp.pad(table, ((0, 0), (0, 0), (0, padded_rows - rows), (0, 0)))
        table = table.reshape(per_dev, lat_parts, HALF, 2, degrees).transpose(0, 3, 1, 2, 4)
        return table.reshape(per_dev, 2, lat_parts * HALF, degrees)

    analysis = banded(jnp.transpose(legendre_analysis, (0, 2, 1)))
    synthesis = banded(legendre_synthesis)
    analysis, first, last = lax.optimization_barrier((analysis, first, last))
    back = spectral(
        gathered, analysis, synthesis, spectral_mixing_weight, jnp.asarray(spread_last(lat_parts))
    )
    back, low, high = lax.optimization_barrier((back, low, high))
    returned = exchange(back)

    tile_rows, tile_cols = ocean_tile_mask.shape
    mask = jnp.pad(ocean_tile_mask, ((0, 8 - tile_rows), (0, 8 - tile_cols)))
    taps = depthwise_filter.reshape(ocean_ch, -1).astype(F32)
    taps = jnp.pad(taps, ((0, -ocean_ch % 8), (0, 0)))
    ocean_next = ocean_block(
        sea,
        forcing,
        odd,
        even,
        low,
        high,
        taps,
        norm_gain_vector[:, None],
        expand_matrix,
        contract_matrix,
        mask,
        (rows // tile_rows, cols // tile_cols),
        reach,
    )

    atmos_next = inverse(returned, table_inv, swap_in, x, gain, parts)
    return (jnp.transpose(atmos_next, (1, 0, 2)), jnp.transpose(ocean_next, (1, 0, 2)))


def solution(mesh):
    in_specs = (
        P("chan", "lat", None),
        P("chan"),
        P(("lat", "chan"), None, None),
        P(("lat", "chan"), None, None),
        P(),
        P(None, "chan"),
        P(),
        P(None, "lat", "chan"),
        P("lat", "chan"),
        P(),
        P(),
        P(),
        P(),
    )
    out_specs = (P("chan", "lat", None), P(None, "lat", "chan"))
    return jax.shard_map(body, mesh=mesh, in_specs=in_specs, out_specs=out_specs, check_vma=False)
```

```python
import functools
import math

import jax
import jax.numpy as jnp
import ml_dtypes
import numpy as np
from jax import lax
from jax.experimental import pallas as pl
from jax.experimental.pallas import tpu as pltpu
from jax.sharding import PartitionSpec as P

BF = jnp.bfloat16
F32 = jnp.float32
VMEM = pl.BlockSpec(memory_space=pltpu.VMEM)
NT = (((1,), (1,)), ((), ()))

HALF = 24


def peer_modes(lat_parts, chan_parts, per_dev):
    j, i, mm = np.meshgrid(np.arange(chan_parts), np.arange(lat_parts), np.arange(per_dev), indexing="ij")
    return ((i * chan_parts + j) * per_dev + mm).reshape(lat_parts * chan_parts, per_dev)


def dft_tables(lon_len, modes):
    total = modes.size
    product = np.arange(lon_len)[:, None, None] * modes.T[None]
    angle = np.float32(2.0 * math.pi / lon_len) * (product % lon_len).astype(np.float32)
    cos, sin = np.cos(angle), np.sin(angle)
    factor = np.float32(math.sqrt(2.0 / lon_len))
    forward = np.stack([factor * cos, -factor * sin], axis=2).reshape(lon_len, total * 2)
    back = np.float32(1.0 / math.sqrt(total))
    inverse = np.stack([back * cos, -back * sin], axis=2).reshape(lon_len, total * 2).T
    return forward.astype(ml_dtypes.bfloat16), np.ascontiguousarray(inverse).astype(ml_dtypes.bfloat16)


def row_swap(outer, inner):
    n = outer * inner
    swap = np.zeros((n, n), np.float32)
    o, k = np.meshgrid(np.arange(outer), np.arange(inner), indexing="ij")
    swap[(o * inner + k).ravel(), (k * outer + o).ravel()] = 1.0
    return swap.astype(ml_dtypes.bfloat16)


def dot(a, b, dims=(((1,), (0,)), ((), ()))):
    return lax.dot_general(a, b, dims, preferred_element_type=F32)


ANY = pl.BlockSpec(memory_space=pl.ANY)
SMEM = pl.BlockSpec(memory_space=pltpu.SMEM)
HBM = pl.BlockSpec(memory_space=pltpu.HBM)
BLOCK = 6


def row_groups(rows):
    return [(at, min(BLOCK, rows - at)) for at in range(0, rows, BLOCK)]


def column(row_ref):
    n = row_ref.shape[1]
    rows = jnp.broadcast_to(row_ref[...].astype(F32), (16, n))
    first = lax.broadcasted_iota(jnp.int32, (16, 128), 0) == 0
    return dot(rows.astype(BF), first.astype(F32).astype(BF), (((0,), (0,)), ((), ())))


def pieces_of(rows):
    return [(0, BLOCK), (BLOCK, 3 * BLOCK), (4 * BLOCK, rows - 4 * BLOCK)]


def copy_pieces(source, target, pieces, sems):
    copies = {}
    for k, (at, size) in enumerate(pieces):
        span = pl.ds(at, size)
        copies[at] = pltpu.make_async_copy(source.at[span], target.at[span], sems.at[k])
        copies[at].start()
    return copies


def forward_kernel(
    at_ref, x_ref, sea_ref, gain_ref, table_ref, swap_ref, out_ref,
    x, sea, table, held, out, x_sems, out_sems, sems
):
    rows, ch, lon = x.shape
    peers = held.shape[1]
    groups = row_groups(rows)
    table_copy = pltpu.make_async_copy(table_ref, table, sems.at[1])
    table_copy.start()
    x_copies = copy_pieces(x_ref, x, pieces_of(rows), x_sems)
    sea_copy = pltpu.make_async_copy(sea_ref.at[:, pl.ds(0, 16), :], sea, sems.at[0])
    sea_copy.start()
    table_copy.wait()
    for at, size in groups:
        if at in x_copies:
            x_copies[at].wait()
        y = dot(x[at : at + size].reshape(size * ch, lon), table[...]).astype(BF)
        for a in range(0, size, 2):
            pieces = []
            for rh in range(2):
                for q in range(4):
                    if a + rh < size:
                        pieces.append(y[(a + rh) * ch : (a + rh + 1) * ch, q * peers : (q + 1) * peers])
                    else:
                        pieces.append(jnp.zeros((ch, peers), BF))
            held[(at + a) // 2] = jnp.concatenate(pieces, axis=0).T

    sea_copy.wait()
    own = sea[:, 0, :].astype(F32)
    own = jnp.concatenate([own, jnp.zeros((ch - rows, own.shape[1]), F32)], axis=0)
    wide = pl.cdiv(lon, 128) * 128
    own = jnp.concatenate([own, jnp.zeros((ch, wide - own.shape[1]), F32)], axis=1)
    own = pltpu.roll(own, at_ref[0] * sea.shape[2], 1)[:, :lon].astype(BF)
    y = dot(own, table[...]).astype(BF)
    pieces = [y[:, q * peers : (q + 1) * peers] for q in range(4)]
    pieces.append(column(gain_ref).astype(BF))
    pieces.append(jnp.zeros((3 * ch, peers), BF))
    held[HALF - 1] = jnp.concatenate(pieces, axis=0).T

    out_copies = []
    half = peers * HALF // 2
    for b in range(peers // 16):
        part = held[:, b * 16 : (b + 1) * 16, :].reshape(HALF * 16, held.shape[2])
        span = pl.ds(b * 16 * HALF, 16 * HALF)
        out[span, :] = dot(swap_ref[...], part).astype(BF)
        if (b + 1) * 16 * HALF % half == 0:
            k = len(out_copies)
            span = pl.ds(k * half, half)
            out_copies.append(pltpu.make_async_copy(out.at[span], out_ref.at[span], out_sems.at[k]))
            out_copies[-1].start()
    for copy in out_copies:
        copy.wait()


def forward(at, x, sea, gain, table, swap):
    rows, ch, lon = x.shape
    peers = table.shape[1] // 4
    return pl.pallas_call(
        forward_kernel,
        out_shape=pltpu.HBM((peers * HALF, 8 * ch), BF),
        in_specs=[SMEM, ANY, ANY, VMEM, ANY, VMEM],
        out_specs=ANY,
        scratch_shapes=[
            pltpu.VMEM(x.shape, BF),
            pltpu.VMEM((rows, 16, sea.shape[2]), BF),
            pltpu.VMEM(table.shape, BF),
            pltpu.VMEM((HALF, peers, 8 * ch), BF),
            pltpu.VMEM((peers * HALF, 8 * ch), BF),
            pltpu.SemaphoreType.DMA((3,)),
            pltpu.SemaphoreType.DMA((2,)),
            pltpu.SemaphoreType.DMA((2,)),
        ],
        compiler_params=pltpu.CompilerParams(vmem_limit_bytes=58 << 20),
        cost_estimate=pl.CostEstimate(
            flops=2 * rows * ch * lon * peers * 4, bytes_accessed=14 << 20, transcendentals=0
        ),
        name="dft_forward",
    )(at, x, sea, gain, table, swap)


def spread_last(lat_parts):
    n = lat_parts * HALF
    col = np.arange(n)
    spread = np.zeros((n, n), np.float32)
    spread[col // HALF * HALF + HALF - 1, col] = 1.0
    return spread.astype(ml_dtypes.bfloat16)


def spectral_kernel(
    wire_hbm, analysis_hbm, synthesis_hbm, mix_hbm, spread_hbm, out_ref,
    wire_ref, analysis_ref, synthesis_ref, mix_ref, spread_ref, spec, mixed, gains, out,
    wire_sems, in_sems, sems
):
    size = analysis_ref.shape[2]
    ch = wire_ref.shape[1] // 8
    groups = wire_ref.shape[0] // size
    pairs = (
        (analysis_hbm, analysis_ref), (spread_hbm, spread_ref), (mix_hbm, mix_ref), (synthesis_hbm, synthesis_ref)
    )
    tables = [pltpu.make_async_copy(a, b, in_sems.at[k]) for k, (a, b) in enumerate(pairs)]
    tables[0].start()
    wires = copy_pieces(wire_hbm, wire_ref, [(0, size), (size, 3 * size), (4 * size, (groups - 4) * size)], wire_sems)
    for copy in tables[1:]:
        copy.start()
    tables[0].wait()
    lines = 0.0
    for j in range(groups):
        if j * size in wires:
            wires[j * size].wait()
        turned = wire_ref[j * size : (j + 1) * size, :].T
        for m in range(2):
            total = sum(
                dot(turned[(4 * rh + 2 * m) * ch : (4 * rh + 2 * m + 2) * ch, :], analysis_ref[m, rh])
                for rh in range(2)
            ).astype(BF)
            for k in range(2):
                spec[m, k, j * ch : (j + 1) * ch, :] = total[k * ch : (k + 1) * ch, :]
        gains[j * ch : (j + 1) * ch, :] = turned[4 * ch : 5 * ch, :128]
        lines = lines + turned[: 4 * ch, :].astype(F32)

    for copy in tables[1:]:
        copy.wait()
    lines = dot(lines.astype(BF), spread_ref[...])
    own_row = lax.broadcasted_iota(jnp.int32, (ch, size), 0)
    rr = lax.rem(lax.broadcasted_iota(jnp.int32, (ch, size), 1), HALF)
    real, imag = mix_ref[0], mix_ref[1]
    gain_real = dot(real, gains[...])[:, HALF - 1 : HALF]
    gain_imag = dot(imag, gains[...])[:, HALF - 1 : HALF]
    for m in range(2):
        surface = 0.0
        for rh in range(2):
            both = [
                jnp.sum(
                    jnp.where(own_row == 2 * rr + rh, lines[q * ch : (q + 1) * ch, :], 0.0),
                    axis=0,
                    keepdims=True,
                )
                for q in (2 * m, 2 * m + 1)
            ]
            both.append(jnp.zeros((6, size), F32))
            both = jnp.concatenate(both, axis=0).astype(BF)
            surface = surface + dot(both, analysis_ref[m, rh])
        sr, si = surface[0:1, :], surface[1:2, :]
        value = dot(real, spec[m, 0]) - dot(imag, spec[m, 1])
        mixed[m, 0] = (value + (gain_real * sr - gain_imag * si)).astype(BF)
        value = dot(imag, spec[m, 0]) + dot(real, spec[m, 1])
        mixed[m, 1] = (value + (gain_imag * sr + gain_real * si)).astype(BF)

    copies = []
    for j in range(groups):
        pieces = []
        for rh in range(2):
            for m in range(2):
                both = [mixed[m, k, j * ch : (j + 1) * ch, :] for k in range(2)]
                pieces.append(dot(synthesis_ref[m, rh], jnp.concatenate(both, axis=0), NT).astype(BF))
        out[j * size : (j + 1) * size, :] = jnp.concatenate(pieces, axis=1)
        if j % 2:
            span = pl.ds((j - 1) * size, 2 * size)
            copies.append(pltpu.make_async_copy(out.at[span], out_ref.at[span], sems.at[j // 2]))
            copies[-1].start()
    for copy in copies:
        copy.wait()


def spectral(wire, analysis, synthesis, mix, spread):
    _, _, size, degrees = analysis.shape
    groups = wire.shape[0] // size
    all_ch = mix.shape[1]
    return pl.pallas_call(
        spectral_kernel,
        out_shape=pltpu.HBM(wire.shape, BF),
        in_specs=[ANY] * 5,
        out_specs=ANY,
        scratch_shapes=[
            *(pltpu.VMEM(a.shape, BF) for a in (wire, analysis, synthesis, mix, spread)),
            pltpu.VMEM((2, 2, all_ch, degrees), BF),
            pltpu.VMEM((2, 2, all_ch, degrees), BF),
            pltpu.VMEM((all_ch, 128), BF),
            pltpu.VMEM(wire.shape, BF),
            pltpu.SemaphoreType.DMA((groups,)),
            pltpu.SemaphoreType.DMA((4,)),
            pltpu.SemaphoreType.DMA((groups,)),
        ],
        compiler_params=pltpu.CompilerParams(vmem_limit_bytes=56 << 20),
        cost_estimate=pl.CostEstimate(flops=2 << 30, bytes_accessed=9 << 20, transcendentals=0),
        name="spectral",
    )(wire, analysis, synthesis, mix, spread)


def inverse_kernel(
    wire_ref, table_ref, swap_ref, x_ref, gain_ref, parts_ref, out_ref,
    wire, table, held, x, out, lines, wire_sems, x_sems, out_sems, sems
):
    rows, ch, lon = x.shape
    peers = held.shape[1]
    groups = row_groups(rows)
    turn = 16 * HALF
    wires = copy_pieces(wire_ref, wire, [(0, 2 * turn), (2 * turn, peers * HALF - 2 * turn)], wire_sems)
    table_copy = pltpu.make_async_copy(table_ref, table, sems.at[0])
    table_copy.start()
    x_copies = copy_pieces(x_ref, x, [(0, rows)], x_sems)
    for b in range(peers // 16):
        if b * turn in wires:
            wires[b * turn].wait()
        part = dot(swap_ref[...], wire[b * turn : (b + 1) * turn, :]).astype(BF)
        held[:, b * 16 : (b + 1) * 16, :] = part.reshape(HALF, 16, held.shape[2])
    chans = parts_ref.shape[0]
    for half in range(2):
        parts = [parts_ref[j, 80:128, :].astype(F32)[SURFACE - 80 : EDGES - 80] for j in range(chans)]
        at = half * PITCH
        lines[half] = jnp.concatenate([part[:, at : at + lon // chans] for part in parts], axis=1)
    gain = column(gain_ref)[:, :1]
    table_copy.wait()

    def wave_of(at, size):
        waves = []
        for a in range(0, size, 2):
            turned = held[(at + a) // 2].T
            for rh in range(min(2, size - a)):
                parts = [turned[(4 * rh + q) * ch : (4 * rh + q + 1) * ch, :] for q in range(4)]
                waves.append(jnp.concatenate(parts, axis=1))
        return dot(jnp.concatenate(waves, axis=0), table[...])

    out_copies = []
    wave = wave_of(*groups[0])
    for g, (at, size) in enumerate(groups):
        if at in x_copies:
            x_copies[at].wait()
        later = wave_of(*groups[g + 1]) if g + 1 < len(groups) else None
        for a in range(size):
            line = lines[a % 2, (at + a) // 2 : (at + a) // 2 + 1, :]
            forced = x[at + a].astype(F32) + gain * line
            out[at + a] = (forced + wave[a * ch : (a + 1) * ch, :]).astype(BF)
        if g % 2 or g + 1 == len(groups):
            span = pl.ds(BLOCK * (g - g % 2), at + size - BLOCK * (g - g % 2))
            out_copies.append(pltpu.make_async_copy(out.at[span], out_ref.at[span], out_sems.at[g]))
            out_copies[-1].start()
        wave = later
    for copy in out_copies:
        copy.wait()


def inverse(wire, table, swap, x, gain, parts):
    rows, ch, lon = x.shape
    peers = table.shape[0] // 4
    groups = len(row_groups(rows))
    return pl.pallas_call(
        inverse_kernel,
        out_shape=pltpu.HBM(x.shape, BF),
        in_specs=[ANY, ANY, VMEM, ANY, VMEM, VMEM],
        out_specs=ANY,
        scratch_shapes=[
            pltpu.VMEM(wire.shape, BF),
            pltpu.VMEM(table.shape, BF),
            pltpu.VMEM((HALF, peers, 8 * ch), BF),
            pltpu.VMEM(x.shape, BF),
            pltpu.VMEM(x.shape, BF),
            pltpu.VMEM((2, HALF, lon), F32),
            pltpu.SemaphoreType.DMA((peers // 16,)),
            pltpu.SemaphoreType.DMA((groups,)),
            pltpu.SemaphoreType.DMA((groups,)),
            pltpu.SemaphoreType.DMA((1,)),
        ],
        compiler_params=pltpu.CompilerParams(vmem_limit_bytes=56 << 20),
        cost_estimate=pl.CostEstimate(
            flops=2 * rows * ch * lon * peers * 4, bytes_accessed=20 << 20, transcendentals=0
        ),
        name="dft_inverse",
    )(wire, table, swap, x, gain, parts)


PITCH = 192


SURFACE = 92
EDGES = SURFACE + HALF
PILE = 9


def flux_kernel(
    reach, at_ref, x_ref, sea_ref, weight_ref, parts_ref, x, sea, out_ref, x_sems, sems
):
    rows, ch, lon = x.shape
    _, oc, cols = sea.shape
    peers = out_ref.shape[0]
    tile = lon // peers
    block = 16
    x_copies = {}
    for k, (at, size) in enumerate([(0, block), (block, block), (2 * block, rows - 2 * block)]):
        span = pl.ds(at, size)
        x_copies[at] = pltpu.make_async_copy(x_ref.at[span], x.at[span], x_sems.at[k])
    sea_copy = pltpu.make_async_copy(sea_ref, sea, sems.at[0])
    x_copies[0].start()
    sea_copy.start()
    x_copies[block].start()
    x_copies[2 * block].start()

    def columns():
        sea_copy.wait()
        own = jnp.concatenate([sea[:, 0, :].astype(F32), jnp.zeros((ch - rows, tile), F32)], axis=0)
        halves = []
        for half in range(2):
            pick = lax.broadcasted_iota(jnp.int32, (HALF, ch), 1) == (
                2 * lax.broadcasted_iota(jnp.int32, (HALF, ch), 0) + half
            )
            halves.append(dot(pick.astype(F32).astype(BF), own.astype(BF)))
            halves.append(jnp.zeros((HALF, PITCH - tile), F32))
        own = jnp.concatenate(halves, axis=1)

        row = lax.broadcasted_iota(jnp.int32, (16, cols), 0)
        col = lax.broadcasted_iota(jnp.int32, (16, cols), 1)
        want = jnp.where(row % 8 < 2 * reach, row % 8 % reach + row // 8 * (cols - reach), -1)
        picks = [
            ((col == want) & (row % 8 // reach == half)).astype(F32).astype(BF) for half in range(2)
        ]
        piles = [[], []]
        for s in range(pl.cdiv(rows, 2)):
            value = dot(picks[0], sea[2 * s], NT)
            if 2 * s + 1 < rows:
                value = value + dot(picks[1], sea[2 * s + 1], NT)
            for half in range(min(2, rows - 2 * s)):
                for k in range(2):
                    piles[k].append(value[8 * k + half * reach : 8 * k + half * reach + reach])
        edges = []
        for pile in piles:
            wide = [jnp.concatenate(pile[k : k + PILE], axis=0) for k in range(0, rows, PILE)]
            wide.append(jnp.zeros((PILE * reach, 2 * PITCH - oc * len(wide)), F32))
            edges.append(jnp.concatenate(wide, axis=1))
        no_edge = jnp.zeros_like(edges[0])
        return own, edges, no_edge

    weight = weight_ref[...].astype(F32)
    weight = jnp.concatenate([weight] * block, axis=1)
    weight = jnp.concatenate([weight] * block, axis=0)
    row = lax.broadcasted_iota(jnp.int32, weight.shape, 0)
    col = lax.broadcasted_iota(jnp.int32, weight.shape, 1)
    keep = col // ch == row % (2 * block) // 4 * 2 + row // (2 * block)
    weight = jnp.where(keep, weight, 0.0).astype(BF)
    before = jnp.zeros((4 * block, reach), BF)
    after = jnp.zeros((4 * block, PITCH - tile - reach), BF)
    out_copies = []
    for at in range(0, rows, block):
        size = min(block, rows - at)
        if at == block:
            own, edges, no_edge = columns()
        if at in x_copies:
            x_copies[at].wait()
        y = dot(weight[:, : size * ch], x[at : at + size].reshape(size * ch, lon)).astype(BF)
        y = jnp.concatenate([before, y, after], axis=1)
        for j in range(peers):
            part = y[:, tile * j : tile * j + PITCH]
            part = jnp.concatenate([part[: 2 * block], part[2 * block :]], axis=1)
            if at + block < rows:
                out_ref[j, 2 * at : 2 * at + 2 * block, :] = part
            else:
                edge = jnp.where(at_ref[0] == j - 1, edges[1], no_edge)
                edge = jnp.where(at_ref[0] == j + 1, edges[0], edge)
                end = out_ref.shape[1] - EDGES - PILE * reach
                part = [part.astype(F32)[: SURFACE - 2 * at], own, edge, jnp.zeros((end, 2 * PITCH), F32)]
                out_ref[j, 2 * at :, :] = jnp.concatenate(part, axis=0).astype(BF)
        if at > 0:
            span = pl.ds(0, 4 * block) if at == block else pl.ds(4 * block, out_ref.shape[1] - 4 * block)
            out_copies.append(
                pltpu.make_async_copy(
                    out_ref.at[:, span], parts_ref.at[:, span], sems.at[1 + len(out_copies)]
                )
            )
            out_copies[-1].start()
    for copy in out_copies:
        copy.wait()


def flux_parts(at, x, sea, weight, reach, peers):
    return pl.pallas_call(
        functools.partial(flux_kernel, reach),
        out_shape=jax.ShapeDtypeStruct((peers, 144, 2 * PITCH), BF),
        in_specs=[SMEM, ANY, ANY, VMEM],
        out_specs=ANY,
        scratch_shapes=[
            pltpu.VMEM(x.shape, BF),
            pltpu.VMEM(sea.shape, BF),
            pltpu.VMEM((peers, 144, 2 * PITCH), BF),
            pltpu.SemaphoreType.DMA((3,)),
            pltpu.SemaphoreType.DMA((3,)),
        ],
        compiler_params=pltpu.CompilerParams(vmem_limit_bytes=58 << 20),
        cost_estimate=pl.CostEstimate(flops=1 << 30, bytes_accessed=7 << 20, transcendentals=0),
        name="flux_parts",
    )(at, x, sea, weight)


def edge_picks(reach, span):
    picks = np.zeros((16, 2 * PITCH), np.float32)
    for side in range(2):
        for half in range(2):
            for dx in range(reach):
                picks[8 * side + reach * half + dx, PITCH * half + side * (span - reach) + dx] = 1.0
    return picks.astype(ml_dtypes.bfloat16)


def pair_forcing(s, left_ref, right_ref, picks, flux, force):
    high = flux.astype(BF).astype(F32)
    low = flux - high
    flux = jnp.concatenate([high, low, high, jnp.zeros_like(high)], axis=0).astype(BF)
    edge = jnp.concatenate([left_ref[s], right_ref[s]], axis=0).astype(BF)
    return dot(
        jnp.concatenate([edge, force], axis=0),
        jnp.concatenate([picks, flux], axis=0),
        (((0,), (0,)), ((), ())),
    )


def pair_rows(first, second, reach):
    ch, cols = first.shape
    before = jnp.zeros((ch, reach), F32)
    after = jnp.zeros((ch, PITCH - cols - reach), F32)
    first, second = first.astype(F32), second.astype(F32)
    return jnp.concatenate([before, first, after, before, second, after], axis=1)


def wet_kernel(
    reach, at_ref, center_ref, picks_ref, parts_ref, force_ref,
    odd_ref, even_ref, forcing_ref, first_ref, last_ref, flux, left_ref, right_ref
):
    rows, ch, _ = center_ref.shape
    own_pairs = odd_ref.shape[0]
    peers = parts_ref.shape[0]
    picks, force = picks_ref[...], force_ref[...]
    total = parts_ref[0, :96, :].astype(F32)
    for j in range(1, peers):
        total = total + parts_ref[j, :96, :].astype(F32)
    at = at_ref[0]
    left = parts_ref[jnp.maximum(at - 1, 0), 112:, :].astype(F32)[EDGES - 112 :]
    right = parts_ref[jnp.minimum(at + 1, peers - 1), 112:, :].astype(F32)[EDGES - 112 :]
    for s in range(own_pairs):
        flux[s] = total[4 * s : 4 * s + 4, :]
        for edge, ref in ((left, left_ref), (right, right_ref)):
            both = []
            for r in (2 * s, 2 * s + 1):
                if r < rows:
                    lanes = slice(ch * (r // PILE), ch * (r // PILE) + ch)
                    both.append(edge[reach * (r % PILE) : reach * (r % PILE) + reach, lanes])
            both.append(jnp.zeros((8 - reach * len(both), ch), F32))
            ref[s] = jnp.concatenate(both, axis=0)

    def fill(s, second):
        more = pair_forcing(s, left_ref, right_ref, picks, flux[s], force)
        forcing_ref[s] = pltpu.roll(more, 2 * PITCH - reach, 1)
        odd_ref[s] = (pair_rows(center_ref[2 * s], second, reach) + more).astype(BF)

    def fill_pair(s, carry):
        fill(s, center_ref[2 * s + 1])
        return carry

    def join(s, carry):
        even_ref[s] = jnp.concatenate([odd_ref[s][:, PITCH:], odd_ref[s + 1][:, :PITCH]], axis=1)
        return carry

    lax.fori_loop(0, own_pairs - 1, fill_pair, 0)
    fill(own_pairs - 1, center_ref[rows - 1])
    lax.fori_loop(0, own_pairs - 1, join, 0)
    even_ref[own_pairs - 1] = odd_ref[own_pairs - 1]
    for at, ref in ((0, first_ref), (rows - reach, last_ref)):
        for d in range(reach):
            half = (at + d) % 2
            ref[d] = odd_ref[(at + d) // 2][:, half * PITCH : (half + 1) * PITCH]


def wet_rows(at, center, picks, parts, force, reach):
    rows, ch, _ = center.shape
    edge = jax.ShapeDtypeStruct((reach, ch, PITCH), BF)
    pairs = (rows + 1) // 2
    own = jax.ShapeDtypeStruct((pairs, ch, 2 * PITCH), BF)
    return pl.pallas_call(
        functools.partial(wet_kernel, reach),
        out_shape=(own, own, jax.ShapeDtypeStruct(own.shape, F32), edge, edge),
        in_specs=[SMEM] + [VMEM] * 4,
        out_specs=(VMEM,) * 5,
        scratch_shapes=[
            pltpu.VMEM((pairs, 4, 2 * PITCH), F32),
            pltpu.VMEM((pairs, 8, ch), F32),
            pltpu.VMEM((pairs, 8, ch), F32),
        ],
        compiler_params=pltpu.CompilerParams(vmem_limit_bytes=24 << 20),
        cost_estimate=pl.CostEstimate(flops=1 << 20, bytes_accessed=1 << 20, transcendentals=0),
        name="wet_rows",
    )(at, center, picks, parts, force)


def ocean_kernel(
    reach, mask_tiles, center_ref, forcing_ref, odd_ref, even_ref, low_ref, high_ref, taps_ref, gain_ref,
    expand_ref, contract_ref, mask_ref, out_ref, odd, even, taps, gain, flag, smooth
):
    step = pl.program_id(0)
    _, ch, cols = center_ref.shape
    high_ch, wide = even.shape[1:]
    pairs = smooth.shape[0]
    side = 2 * reach + 1
    own_pairs = odd_ref.shape[0]

    @pl.when(step == 0)
    def _():
        def widen(s, carry):
            odd[s + 2, :ch, :] = odd_ref[s].astype(F32)
            even[s + 2, :ch, :] = even_ref[s].astype(F32)
            return carry

        lax.fori_loop(0, own_pairs, widen, 0)
        odd[0, :ch, PITCH:] = low_ref[0].astype(F32)
        odd[1, :ch, :] = jnp.concatenate([low_ref[1].astype(F32), low_ref[2].astype(F32)], axis=1)
        odd[own_pairs + 1, :ch, PITCH:] = high_ref[0].astype(F32)
        odd[own_pairs + 2, :ch, :] = jnp.concatenate(
            [high_ref[1].astype(F32), high_ref[2].astype(F32)], axis=1
        )
        for t in (0, 1, own_pairs + 1, own_pairs + 2):
            even[t] = jnp.concatenate([odd[t][:, PITCH:], odd[t + 1][:, :PITCH]], axis=1)
        for k in range(side * side):
            taps[k] = jnp.broadcast_to(taps_ref[:, k : k + 1], taps.shape[1:])
        gain[...] = jnp.broadcast_to(gain_ref[...], gain.shape)
        tall, across = mask_tiles
        mask = mask_ref[...].astype(F32).astype(BF)
        spread = 0.0
        for half in range(2):
            pair = lax.broadcasted_iota(jnp.int32, (32, 8), 0)
            tile = lax.broadcasted_iota(jnp.int32, (32, 8), 1)
            up = ((2 * pair + half) // tall == tile).astype(F32).astype(BF)
            lane = lax.broadcasted_iota(jnp.int32, (8, wide), 1) - half * PITCH
            tile = lax.broadcasted_iota(jnp.int32, (8, wide), 0)
            side_by = (lane >= 0) & (lane < cols) & (lane // across == tile)
            side_by = side_by.astype(F32).astype(BF)
            spread = spread + dot(dot(up, mask).astype(BF), side_by)
        for s in range(flag.shape[0]):
            flag[s] = jnp.broadcast_to(spread[s : s + 1, :], (8, wide))

    start = step * pairs

    def channels(c, carry):
        at = pl.multiple_of(c * 8, 8)
        total = [None] * pairs
        for dx in range(side):
            part = [None] * pairs
            for dy in range(side):
                tap = taps[dy * side + dx, pl.ds(at, 8), :]
                tap = jnp.concatenate([tap] * (wide // 128), axis=1)
                for p in range(pairs):
                    if dy % 2 == 0:
                        value = even[start + p + dy // 2, pl.ds(at, 8), :]
                    else:
                        value = odd[start + p + dy // 2 + 1, pl.ds(at, 8), :]
                    term = tap * value
                    part[p] = term if part[p] is None else part[p] + term
            for p in range(pairs):
                moved = part[p] if dx == 0 else pltpu.roll(part[p], wide - dx, 1)
                total[p] = moved if total[p] is None else total[p] + moved
        for p in range(pairs):
            smooth[p, pl.ds(at, 8), :] = total[p]
        return carry

    lax.fori_loop(0, high_ch // 8, channels, 0)
    scale = jnp.concatenate([gain[...]] * (wide // 128), axis=1)
    for p in range(pairs):
        value = smooth[p, :ch, :]
        value = value - jnp.mean(value, axis=0, keepdims=True)
        spread = jnp.mean(value * value, axis=0, keepdims=True)
        normed = (value * lax.rsqrt(spread + 1e-06) * scale).astype(BF)
        hidden = dot(expand_ref[...], normed)
        inner = hidden * (0.7978845608028654 + 0.035677408136300125 * (hidden * hidden))
        hidden = (hidden + hidden * jnp.tanh(inner)).astype(BF)
        branch = 0.5 * dot(contract_ref[...], hidden)
        change = flag[start + p][:1] * (forcing_ref[p] + branch)
        for half in range(2):
            moved = change[:, half * PITCH : half * PITCH + cols]
            out_ref[2 * p + half] = (center_ref[2 * p + half].astype(F32) + moved).astype(BF)


def ocean_block(
    center, forcing, odd, even, low, high, taps, gain, expand, contract, mask, mask_tiles, reach
):
    rows, ch, cols = center.shape
    pairs = 6
    steps = pl.cdiv((rows + 1) // 2, pairs)
    high_ch = pl.cdiv(ch, 8) * 8
    deep = steps * pairs + reach + 1
    whole = lambda a: pl.BlockSpec(a.shape, lambda g: (0,) * a.ndim)
    operands = (center, forcing, odd, even, low, high, taps, gain, expand, contract, mask)
    return pl.pallas_call(
        functools.partial(ocean_kernel, reach, mask_tiles),
        out_shape=jax.ShapeDtypeStruct(center.shape, BF),
        grid=(steps,),
        in_specs=[
            pl.BlockSpec((2 * pairs, ch, cols), lambda g: (g, 0, 0)),
            pl.BlockSpec((pairs, ch, 2 * PITCH), lambda g: (g, 0, 0)),
            *(whole(a) for a in operands[2:]),
        ],
        out_specs=pl.BlockSpec((2 * pairs, ch, cols), lambda g: (g, 0, 0)),
        scratch_shapes=[
            pltpu.VMEM((deep, high_ch, 2 * PITCH), F32),
            pltpu.VMEM((deep, high_ch, 2 * PITCH), F32),
            pltpu.VMEM((taps.shape[1], high_ch, 128), F32),
            pltpu.VMEM((ch, 128), F32),
            pltpu.VMEM((steps * pairs, 8, 2 * PITCH), F32),
            pltpu.VMEM((pairs, high_ch, 2 * PITCH), F32),
        ],
        compiler_params=pltpu.CompilerParams(vmem_limit_bytes=32 << 20),
        cost_estimate=pl.CostEstimate(
            flops=30 << 30, bytes_accessed=8 << 20, transcendentals=3 << 20
        ),
        name="ocean_block",
    )(*operands)


def shift(first, last, axis):
    count = lax.axis_size(axis)
    up = [(i, i + 1) for i in range(count - 1)]
    down = [(target, source) for source, target in up]
    return lax.ppermute(last, axis, up), lax.ppermute(first, axis, down)


def body(
    atmos,
    sea_temp_gain,
    legendre_analysis,
    legendre_synthesis,
    spectral_mixing_weight,
    surface_flux_weight,
    flux_ocean_forcing,
    ocean,
    ocean_tile_mask,
    depthwise_filter,
    norm_gain_vector,
    expand_matrix,
    contract_matrix,
):
    lat_parts = lax.axis_size("lat")
    chan_parts = lax.axis_size("chan")
    chan_at = lax.axis_index("chan")
    ch, rows, lon = atmos.shape
    per_dev, degrees, _ = legendre_analysis.shape
    ocean_ch, _, cols = ocean.shape
    reach = depthwise_filter.shape[2] // 2
    peers = lat_parts * chan_parts
    padded_rows = 2 * HALF

    table_fwd, table_inv = dft_tables(lon, peer_modes(lat_parts, chan_parts, per_dev))
    table_fwd, table_inv = jnp.asarray(table_fwd), jnp.asarray(table_inv)
    swap_out = jnp.asarray(row_swap(16, HALF))
    swap_in = jnp.asarray(row_swap(HALF, 16))

    x = jnp.transpose(atmos, (1, 0, 2))
    sea = jnp.transpose(ocean, (1, 0, 2))

    def exchange(wire):
        return lax.all_to_all(
            wire.reshape(peers, HALF, 8 * ch), ("chan", "lat"), 0, 0, tiled=True
        ).reshape(wire.shape)

    at = jnp.reshape(chan_at, (1,)).astype(jnp.int32)
    parts = flux_parts(at, x, sea, surface_flux_weight, reach, chan_parts)
    parts = lax.all_to_all(parts, "chan", 0, 0, tiled=True)

    gain = sea_temp_gain[None]
    wire = forward(at, x, sea, gain, table_fwd, swap_out)
    gathered = exchange(wire)
    sea, legendre_analysis, legendre_synthesis, wire = lax.optimization_barrier(
        (sea, legendre_analysis, legendre_synthesis, wire)
    )
    force = flux_ocean_forcing.T
    force_high = force.astype(BF)
    force_low = (force - force_high.astype(F32)).astype(BF)
    force = jnp.concatenate([force_high, force_high, force_low, jnp.zeros_like(force_low)], axis=0)
    picks = jnp.asarray(edge_picks(reach, cols + 2 * reach))
    odd, even, forcing, first, last = wet_rows(at, sea, picks, parts, force, reach)
    low, high = shift(first, last, "lat")

    def banded(table):
        table = table.reshape(per_dev, lat_parts, rows, degrees)
        table = jnp.pad(table, ((0, 0), (0, 0), (0, padded_rows - rows), (0, 0)))
        table = table.reshape(per_dev, lat_parts, HALF, 2, degrees).transpose(0, 3, 1, 2, 4)
        return table.reshape(per_dev, 2, lat_parts * HALF, degrees)

    analysis = banded(jnp.transpose(legendre_analysis, (0, 2, 1)))
    synthesis = banded(legendre_synthesis)
    analysis, first, last = lax.optimization_barrier((analysis, first, last))
    back = spectral(
        gathered, analysis, synthesis, spectral_mixing_weight, jnp.asarray(spread_last(lat_parts))
    )
    back, low, high = lax.optimization_barrier((back, low, high))
    returned = exchange(back)

    tile_rows, tile_cols = ocean_tile_mask.shape
    mask = jnp.pad(ocean_tile_mask, ((0, 8 - tile_rows), (0, 8 - tile_cols)))
    taps = depthwise_filter.reshape(ocean_ch, -1).astype(F32)
    taps = jnp.pad(taps, ((0, -ocean_ch % 8), (0, 0)))
    ocean_next = ocean_block(
        sea,
        forcing,
        odd,
        even,
        low,
        high,
        taps,
        norm_gain_vector[:, None],
        expand_matrix,
        contract_matrix,
        mask,
        (rows // tile_rows, cols // tile_cols),
        reach,
    )

    atmos_next = inverse(returned, table_inv, swap_in, x, gain, parts)
    return (jnp.transpose(atmos_next, (1, 0, 2)), jnp.transpose(ocean_next, (1, 0, 2)))


def solution(mesh):
    in_specs = (
        P("chan", "lat", None),
        P("chan"),
        P(("lat", "chan"), None, None),
        P(("lat", "chan"), None, None),
        P(),
        P(None, "chan"),
        P(),
        P(None, "lat", "chan"),
        P("lat", "chan"),
        P(),
        P(),
        P(),
        P(),
    )
    out_specs = (P("chan", "lat", None), P(None, "lat", "chan"))
    return jax.shard_map(body, mesh=mesh, in_specs=in_specs, out_specs=out_specs, check_vma=False)
```

```python
import functools
import math

import jax
import jax.numpy as jnp
import ml_dtypes
import numpy as np
from jax import lax
from jax.experimental import pallas as pl
from jax.experimental.pallas import tpu as pltpu
from jax.sharding import PartitionSpec as P

BF = jnp.bfloat16
F32 = jnp.float32
VMEM = pl.BlockSpec(memory_space=pltpu.VMEM)
NT = (((1,), (1,)), ((), ()))

HALF = 24


def peer_modes(lat_parts, chan_parts, per_dev):
    j, i, mm = np.meshgrid(np.arange(chan_parts), np.arange(lat_parts), np.arange(per_dev), indexing="ij")
    return ((i * chan_parts + j) * per_dev + mm).reshape(lat_parts * chan_parts, per_dev)


def dft_tables(lon_len, modes):
    total = modes.size
    product = np.arange(lon_len)[:, None, None] * modes.T[None]
    angle = np.float32(2.0 * math.pi / lon_len) * (product % lon_len).astype(np.float32)
    cos, sin = np.cos(angle), np.sin(angle)
    factor = np.float32(math.sqrt(2.0 / lon_len))
    forward = np.stack([factor * cos, -factor * sin], axis=2).reshape(lon_len, total * 2)
    back = np.float32(1.0 / math.sqrt(total))
    inverse = np.stack([back * cos, -back * sin], axis=2).reshape(lon_len, total * 2).T
    return forward.astype(ml_dtypes.bfloat16), np.ascontiguousarray(inverse).astype(ml_dtypes.bfloat16)


def row_swap(outer, inner):
    n = outer * inner
    swap = np.zeros((n, n), np.float32)
    o, k = np.meshgrid(np.arange(outer), np.arange(inner), indexing="ij")
    swap[(o * inner + k).ravel(), (k * outer + o).ravel()] = 1.0
    return swap.astype(ml_dtypes.bfloat16)


def dot(a, b, dims=(((1,), (0,)), ((), ()))):
    return lax.dot_general(a, b, dims, preferred_element_type=F32)


ANY = pl.BlockSpec(memory_space=pl.ANY)
SMEM = pl.BlockSpec(memory_space=pltpu.SMEM)
HBM = pl.BlockSpec(memory_space=pltpu.HBM)
BLOCK = 6


def row_groups(rows):
    return [(at, min(BLOCK, rows - at)) for at in range(0, rows, BLOCK)]


def column(row_ref):
    n = row_ref.shape[1]
    rows = jnp.broadcast_to(row_ref[...].astype(F32), (16, n))
    first = lax.broadcasted_iota(jnp.int32, (16, 128), 0) == 0
    return dot(rows.astype(BF), first.astype(F32).astype(BF), (((0,), (0,)), ((), ())))


def pieces_of(rows):
    return [(0, BLOCK), (BLOCK, 3 * BLOCK), (4 * BLOCK, rows - 4 * BLOCK)]


def copy_pieces(source, target, pieces, sems):
    copies = {}
    for k, (at, size) in enumerate(pieces):
        span = pl.ds(at, size)
        copies[at] = pltpu.make_async_copy(source.at[span], target.at[span], sems.at[k])
        copies[at].start()
    return copies


def forward_kernel(
    at_ref, x_ref, sea_ref, gain_ref, table_ref, swap_ref, out_ref,
    x, sea, table, held, out, x_sems, out_sems, sems
):
    rows, ch, lon = x.shape
    peers = held.shape[1]
    groups = row_groups(rows)
    table_copy = pltpu.make_async_copy(table_ref, table, sems.at[1])
    table_copy.start()
    x_copies = copy_pieces(x_ref, x, pieces_of(rows), x_sems)
    sea_copy = pltpu.make_async_copy(sea_ref.at[:, pl.ds(0, 16), :], sea, sems.at[0])
    sea_copy.start()
    table_copy.wait()
    for at, size in groups:
        if at in x_copies:
            x_copies[at].wait()
        y = dot(x[at : at + size].reshape(size * ch, lon), table[...]).astype(BF)
        for a in range(0, size, 2):
            pieces = []
            for rh in range(2):
                for q in range(4):
                    if a + rh < size:
                        pieces.append(y[(a + rh) * ch : (a + rh + 1) * ch, q * peers : (q + 1) * peers])
                    else:
                        pieces.append(jnp.zeros((ch, peers), BF))
            held[(at + a) // 2] = jnp.concatenate(pieces, axis=0).T

    sea_copy.wait()
    own = sea[:, 0, :].astype(F32)
    own = jnp.concatenate([own, jnp.zeros((ch - rows, own.shape[1]), F32)], axis=0)
    wide = pl.cdiv(lon, 128) * 128
    own = jnp.concatenate([own, jnp.zeros((ch, wide - own.shape[1]), F32)], axis=1)
    own = pltpu.roll(own, at_ref[0] * sea.shape[2], 1)[:, :lon].astype(BF)
    y = dot(own, table[...]).astype(BF)
    pieces = [y[:, q * peers : (q + 1) * peers] for q in range(4)]
    pieces.append(column(gain_ref).astype(BF))
    pieces.append(jnp.zeros((3 * ch, peers), BF))
    held[HALF - 1] = jnp.concatenate(pieces, axis=0).T

    out_copies = []
    half = peers * HALF // 2
    for b in range(peers // 16):
        part = held[:, b * 16 : (b + 1) * 16, :].reshape(HALF * 16, held.shape[2])
        span = pl.ds(b * 16 * HALF, 16 * HALF)
        out[span, :] = dot(swap_ref[...], part).astype(BF)
        if (b + 1) * 16 * HALF % half == 0:
            k = len(out_copies)
            span = pl.ds(k * half, half)
            out_copies.append(pltpu.make_async_copy(out.at[span], out_ref.at[span], out_sems.at[k]))
            out_copies[-1].start()
    for copy in out_copies:
        copy.wait()


def forward(at, x, sea, gain, table, swap):
    rows, ch, lon = x.shape
    peers = table.shape[1] // 4
    return pl.pallas_call(
        forward_kernel,
        out_shape=pltpu.HBM((peers * HALF, 8 * ch), BF),
        in_specs=[SMEM, ANY, ANY, VMEM, ANY, VMEM],
        out_specs=ANY,
        scratch_shapes=[
            pltpu.VMEM(x.shape, BF),
            pltpu.VMEM((rows, 16, sea.shape[2]), BF),
            pltpu.VMEM(table.shape, BF),
            pltpu.VMEM((HALF, peers, 8 * ch), BF),
            pltpu.VMEM((peers * HALF, 8 * ch), BF),
            pltpu.SemaphoreType.DMA((3,)),
            pltpu.SemaphoreType.DMA((2,)),
            pltpu.SemaphoreType.DMA((2,)),
        ],
        compiler_params=pltpu.CompilerParams(vmem_limit_bytes=58 << 20),
        cost_estimate=pl.CostEstimate(
            flops=2 * rows * ch * lon * peers * 4, bytes_accessed=14 << 20, transcendentals=0
        ),
        name="dft_forward",
    )(at, x, sea, gain, table, swap)


def spread_last(lat_parts):
    n = lat_parts * HALF
    col = np.arange(n)
    spread = np.zeros((n, n), np.float32)
    spread[col // HALF * HALF + HALF - 1, col] = 1.0
    return spread.astype(ml_dtypes.bfloat16)


def spectral_kernel(
    wire_hbm, analysis_hbm, synthesis_hbm, mix_hbm, spread_hbm, out_ref,
    wire_ref, analysis_ref, synthesis_ref, mix_ref, spread_ref, spec, mixed, gains, out,
    wire_sems, in_sems, sems
):
    size = analysis_ref.shape[2]
    ch = wire_ref.shape[1] // 8
    groups = wire_ref.shape[0] // size
    pairs = (
        (analysis_hbm, analysis_ref), (spread_hbm, spread_ref), (mix_hbm, mix_ref), (synthesis_hbm, synthesis_ref)
    )
    tables = [pltpu.make_async_copy(a, b, in_sems.at[k]) for k, (a, b) in enumerate(pairs)]
    tables[0].start()
    wires = copy_pieces(wire_hbm, wire_ref, [(0, size), (size, 3 * size), (4 * size, (groups - 4) * size)], wire_sems)
    for copy in tables[1:]:
        copy.start()
    tables[0].wait()
    lines = 0.0
    for j in range(groups):
        if j * size in wires:
            wires[j * size].wait()
        turned = wire_ref[j * size : (j + 1) * size, :].T
        for m in range(2):
            total = sum(
                dot(turned[(4 * rh + 2 * m) * ch : (4 * rh + 2 * m + 2) * ch, :], analysis_ref[m, rh])
                for rh in range(2)
            ).astype(BF)
            for k in range(2):
                spec[m, k, j * ch : (j + 1) * ch, :] = total[k * ch : (k + 1) * ch, :]
        gains[j * ch : (j + 1) * ch, :] = turned[4 * ch : 5 * ch, :128]
        lines = lines + turned[: 4 * ch, :].astype(F32)

    for copy in tables[1:]:
        copy.wait()
    lines = dot(lines.astype(BF), spread_ref[...])
    own_row = lax.broadcasted_iota(jnp.int32, (ch, size), 0)
    rr = lax.rem(lax.broadcasted_iota(jnp.int32, (ch, size), 1), HALF)
    real, imag = mix_ref[0], mix_ref[1]
    gain_real = dot(real, gains[...])[:, HALF - 1 : HALF]
    gain_imag = dot(imag, gains[...])[:, HALF - 1 : HALF]
    for m in range(2):
        surface = 0.0
        for rh in range(2):
            both = [
                jnp.sum(
                    jnp.where(own_row == 2 * rr + rh, lines[q * ch : (q + 1) * ch, :], 0.0),
                    axis=0,
                    keepdims=True,
                )
                for q in (2 * m, 2 * m + 1)
            ]
            both.append(jnp.zeros((6, size), F32))
            both = jnp.concatenate(both, axis=0).astype(BF)
            surface = surface + dot(both, analysis_ref[m, rh])
        sr, si = surface[0:1, :], surface[1:2, :]
        value = dot(real, spec[m, 0]) - dot(imag, spec[m, 1])
        mixed[m, 0] = (value + (gain_real * sr - gain_imag * si)).astype(BF)
        value = dot(imag, spec[m, 0]) + dot(real, spec[m, 1])
        mixed[m, 1] = (value + (gain_imag * sr + gain_real * si)).astype(BF)

    copies = []
    for j in range(groups):
        pieces = []
        for rh in range(2):
            for m in range(2):
                both = [mixed[m, k, j * ch : (j + 1) * ch, :] for k in range(2)]
                pieces.append(dot(synthesis_ref[m, rh], jnp.concatenate(both, axis=0), NT).astype(BF))
        out[j * size : (j + 1) * size, :] = jnp.concatenate(pieces, axis=1)
        if j % 2:
            span = pl.ds((j - 1) * size, 2 * size)
            copies.append(pltpu.make_async_copy(out.at[span], out_ref.at[span], sems.at[j // 2]))
            copies[-1].start()
    for copy in copies:
        copy.wait()


def spectral(wire, analysis, synthesis, mix, spread):
    _, _, size, degrees = analysis.shape
    groups = wire.shape[0] // size
    all_ch = mix.shape[1]
    return pl.pallas_call(
        spectral_kernel,
        out_shape=pltpu.HBM(wire.shape, BF),
        in_specs=[ANY] * 5,
        out_specs=ANY,
        scratch_shapes=[
            *(pltpu.VMEM(a.shape, BF) for a in (wire, analysis, synthesis, mix, spread)),
            pltpu.VMEM((2, 2, all_ch, degrees), BF),
            pltpu.VMEM((2, 2, all_ch, degrees), BF),
            pltpu.VMEM((all_ch, 128), BF),
            pltpu.VMEM(wire.shape, BF),
            pltpu.SemaphoreType.DMA((groups,)),
            pltpu.SemaphoreType.DMA((4,)),
            pltpu.SemaphoreType.DMA((groups,)),
        ],
        compiler_params=pltpu.CompilerParams(vmem_limit_bytes=56 << 20),
        cost_estimate=pl.CostEstimate(flops=2 << 30, bytes_accessed=9 << 20, transcendentals=0),
        name="spectral",
    )(wire, analysis, synthesis, mix, spread)


def inverse_kernel(
    wire_ref, table_ref, swap_ref, x_ref, gain_ref, parts_ref, out_ref,
    wire, table, held, x, out, lines, wire_sems, x_sems, out_sems, sems
):
    rows, ch, lon = x.shape
    peers = held.shape[1]
    groups = row_groups(rows)
    turn = 16 * HALF
    wires = copy_pieces(wire_ref, wire, [(0, 2 * turn), (2 * turn, peers * HALF - 2 * turn)], wire_sems)
    table_copy = pltpu.make_async_copy(table_ref, table, sems.at[0])
    table_copy.start()
    x_copies = copy_pieces(x_ref, x, [(0, rows)], x_sems)
    for b in range(peers // 16):
        if b * turn in wires:
            wires[b * turn].wait()
        part = dot(swap_ref[...], wire[b * turn : (b + 1) * turn, :]).astype(BF)
        held[:, b * 16 : (b + 1) * 16, :] = part.reshape(HALF, 16, held.shape[2])
    chans = parts_ref.shape[0]
    for half in range(2):
        parts = [parts_ref[j, 80:128, :].astype(F32)[SURFACE - 80 : EDGES - 80] for j in range(chans)]
        at = half * PITCH
        lines[half] = jnp.concatenate([part[:, at : at + lon // chans] for part in parts], axis=1)
    gain = column(gain_ref)[:, :1]
    table_copy.wait()

    def wave_of(at, size):
        waves = []
        for a in range(0, size, 2):
            turned = held[(at + a) // 2].T
            for rh in range(min(2, size - a)):
                parts = [turned[(4 * rh + q) * ch : (4 * rh + q + 1) * ch, :] for q in range(4)]
                waves.append(jnp.concatenate(parts, axis=1))
        return dot(jnp.concatenate(waves, axis=0), table[...])

    out_copies = []
    wave = wave_of(*groups[0])
    for g, (at, size) in enumerate(groups):
        if at in x_copies:
            x_copies[at].wait()
        later = wave_of(*groups[g + 1]) if g + 1 < len(groups) else None
        for a in range(size):
            line = lines[a % 2, (at + a) // 2 : (at + a) // 2 + 1, :]
            forced = x[at + a].astype(F32) + gain * line
            out[at + a] = (forced + wave[a * ch : (a + 1) * ch, :]).astype(BF)
        if g % 2 or g + 1 == len(groups):
            span = pl.ds(BLOCK * (g - g % 2), at + size - BLOCK * (g - g % 2))
            out_copies.append(pltpu.make_async_copy(out.at[span], out_ref.at[span], out_sems.at[g]))
            out_copies[-1].start()
        wave = later
    for copy in out_copies:
        copy.wait()


def inverse(wire, table, swap, x, gain, parts):
    rows, ch, lon = x.shape
    peers = table.shape[0] // 4
    groups = len(row_groups(rows))
    return pl.pallas_call(
        inverse_kernel,
        out_shape=pltpu.HBM(x.shape, BF),
        in_specs=[ANY, ANY, VMEM, ANY, VMEM, VMEM],
        out_specs=ANY,
        scratch_shapes=[
            pltpu.VMEM(wire.shape, BF),
            pltpu.VMEM(table.shape, BF),
            pltpu.VMEM((HALF, peers, 8 * ch), BF),
            pltpu.VMEM(x.shape, BF),
            pltpu.VMEM(x.shape, BF),
            pltpu.VMEM((2, HALF, lon), F32),
            pltpu.SemaphoreType.DMA((peers // 16,)),
            pltpu.SemaphoreType.DMA((groups,)),
            pltpu.SemaphoreType.DMA((groups,)),
            pltpu.SemaphoreType.DMA((1,)),
        ],
        compiler_params=pltpu.CompilerParams(vmem_limit_bytes=56 << 20),
        cost_estimate=pl.CostEstimate(
            flops=2 * rows * ch * lon * peers * 4, bytes_accessed=20 << 20, transcendentals=0
        ),
        name="dft_inverse",
    )(wire, table, swap, x, gain, parts)


PITCH = 192


SURFACE = 92
EDGES = SURFACE + HALF
PILE = 9


def flux_kernel(
    reach, at_ref, x_ref, sea_ref, weight_ref, parts_ref, x, sea, out_ref, x_sems, sems
):
    rows, ch, lon = x.shape
    _, oc, cols = sea.shape
    peers = out_ref.shape[0]
    tile = lon // peers
    block = 16
    x_copies = {}
    for k, (at, size) in enumerate([(0, block), (block, block), (2 * block, rows - 2 * block)]):
        span = pl.ds(at, size)
        x_copies[at] = pltpu.make_async_copy(x_ref.at[span], x.at[span], x_sems.at[k])
    sea_copy = pltpu.make_async_copy(sea_ref, sea, sems.at[0])
    x_copies[0].start()
    sea_copy.start()
    x_copies[block].start()
    x_copies[2 * block].start()

    def columns():
        sea_copy.wait()
        own = jnp.concatenate([sea[:, 0, :].astype(F32), jnp.zeros((ch - rows, tile), F32)], axis=0)
        halves = []
        for half in range(2):
            pick = lax.broadcasted_iota(jnp.int32, (HALF, ch), 1) == (
                2 * lax.broadcasted_iota(jnp.int32, (HALF, ch), 0) + half
            )
            halves.append(dot(pick.astype(F32).astype(BF), own.astype(BF)))
            halves.append(jnp.zeros((HALF, PITCH - tile), F32))
        own = jnp.concatenate(halves, axis=1)

        row = lax.broadcasted_iota(jnp.int32, (16, cols), 0)
        col = lax.broadcasted_iota(jnp.int32, (16, cols), 1)
        want = jnp.where(row % 8 < 2 * reach, row % 8 % reach + row // 8 * (cols - reach), -1)
        picks = [
            ((col == want) & (row % 8 // reach == half)).astype(F32).astype(BF) for half in range(2)
        ]
        piles = [[], []]
        for s in range(pl.cdiv(rows, 2)):
            value = dot(picks[0], sea[2 * s], NT)
            if 2 * s + 1 < rows:
                value = value + dot(picks[1], sea[2 * s + 1], NT)
            for half in range(min(2, rows - 2 * s)):
                for k in range(2):
                    piles[k].append(value[8 * k + half * reach : 8 * k + half * reach + reach])
        edges = []
        for pile in piles:
            wide = [jnp.concatenate(pile[k : k + PILE], axis=0) for k in range(0, rows, PILE)]
            wide.append(jnp.zeros((PILE * reach, 2 * PITCH - oc * len(wide)), F32))
            edges.append(jnp.concatenate(wide, axis=1))
        no_edge = jnp.zeros_like(edges[0])
        return own, edges, no_edge

    weight = weight_ref[...].astype(F32)
    weight = jnp.concatenate([weight] * block, axis=1)
    weight = jnp.concatenate([weight] * block, axis=0)
    row = lax.broadcasted_iota(jnp.int32, weight.shape, 0)
    col = lax.broadcasted_iota(jnp.int32, weight.shape, 1)
    keep = col // ch == row % (2 * block) // 4 * 2 + row // (2 * block)
    weight = jnp.where(keep, weight, 0.0).astype(BF)
    before = jnp.zeros((4 * block, reach), BF)
    after = jnp.zeros((4 * block, PITCH - tile - reach), BF)
    out_copies = []
    for at in range(0, rows, block):
        size = min(block, rows - at)
        if at in x_copies:
            x_copies[at].wait()
        y = dot(weight[:, : size * ch], x[at : at + size].reshape(size * ch, lon)).astype(BF)
        if at == block:
            own, edges, no_edge = columns()
        y = jnp.concatenate([before, y, after], axis=1)
        for j in range(peers):
            part = y[:, tile * j : tile * j + PITCH]
            part = jnp.concatenate([part[: 2 * block], part[2 * block :]], axis=1)
            if at + block < rows:
                out_ref[j, 2 * at : 2 * at + 2 * block, :] = part
            else:
                edge = jnp.where(at_ref[0] == j - 1, edges[1], no_edge)
                edge = jnp.where(at_ref[0] == j + 1, edges[0], edge)
                end = out_ref.shape[1] - EDGES - PILE * reach
                part = [part.astype(F32)[: SURFACE - 2 * at], own, edge, jnp.zeros((end, 2 * PITCH), F32)]
                out_ref[j, 2 * at :, :] = jnp.concatenate(part, axis=0).astype(BF)
        if at > 0:
            span = pl.ds(0, 4 * block) if at == block else pl.ds(4 * block, out_ref.shape[1] - 4 * block)
            out_copies.append(
                pltpu.make_async_copy(
                    out_ref.at[:, span], parts_ref.at[:, span], sems.at[1 + len(out_copies)]
                )
            )
            out_copies[-1].start()
    for copy in out_copies:
        copy.wait()


def flux_parts(at, x, sea, weight, reach, peers):
    return pl.pallas_call(
        functools.partial(flux_kernel, reach),
        out_shape=jax.ShapeDtypeStruct((peers, 144, 2 * PITCH), BF),
        in_specs=[SMEM, ANY, ANY, VMEM],
        out_specs=ANY,
        scratch_shapes=[
            pltpu.VMEM(x.shape, BF),
            pltpu.VMEM(sea.shape, BF),
            pltpu.VMEM((peers, 144, 2 * PITCH), BF),
            pltpu.SemaphoreType.DMA((3,)),
            pltpu.SemaphoreType.DMA((3,)),
        ],
        compiler_params=pltpu.CompilerParams(vmem_limit_bytes=58 << 20),
        cost_estimate=pl.CostEstimate(flops=1 << 30, bytes_accessed=7 << 20, transcendentals=0),
        name="flux_parts",
    )(at, x, sea, weight)


def edge_picks(reach, span):
    picks = np.zeros((16, 2 * PITCH), np.float32)
    for side in range(2):
        for half in range(2):
            for dx in range(reach):
                picks[8 * side + reach * half + dx, PITCH * half + side * (span - reach) + dx] = 1.0
    return picks.astype(ml_dtypes.bfloat16)


def pair_forcing(s, left_ref, right_ref, picks, flux, force):
    high = flux.astype(BF).astype(F32)
    low = flux - high
    flux = jnp.concatenate([high, low, high, jnp.zeros_like(high)], axis=0).astype(BF)
    edge = jnp.concatenate([left_ref[s], right_ref[s]], axis=0).astype(BF)
    return dot(
        jnp.concatenate([edge, force], axis=0),
        jnp.concatenate([picks, flux], axis=0),
        (((0,), (0,)), ((), ())),
    )


def pair_rows(first, second, reach):
    ch, cols = first.shape
    before = jnp.zeros((ch, reach), F32)
    after = jnp.zeros((ch, PITCH - cols - reach), F32)
    first, second = first.astype(F32), second.astype(F32)
    return jnp.concatenate([before, first, after, before, second, after], axis=1)


def wet_kernel(
    reach, at_ref, center_ref, picks_ref, parts_ref, force_ref,
    odd_ref, even_ref, forcing_ref, first_ref, last_ref, flux, left_ref, right_ref
):
    rows, ch, _ = center_ref.shape
    own_pairs = odd_ref.shape[0]
    peers = parts_ref.shape[0]
    picks, force = picks_ref[...], force_ref[...]
    total = parts_ref[0, :96, :].astype(F32)
    for j in range(1, peers):
        total = total + parts_ref[j, :96, :].astype(F32)
    at = at_ref[0]
    left = parts_ref[jnp.maximum(at - 1, 0), 112:, :].astype(F32)[EDGES - 112 :]
    right = parts_ref[jnp.minimum(at + 1, peers - 1), 112:, :].astype(F32)[EDGES - 112 :]
    for s in range(own_pairs):
        flux[s] = total[4 * s : 4 * s + 4, :]
        for edge, ref in ((left, left_ref), (right, right_ref)):
            both = []
            for r in (2 * s, 2 * s + 1):
                if r < rows:
                    lanes = slice(ch * (r // PILE), ch * (r // PILE) + ch)
                    both.append(edge[reach * (r % PILE) : reach * (r % PILE) + reach, lanes])
            both.append(jnp.zeros((8 - reach * len(both), ch), F32))
            ref[s] = jnp.concatenate(both, axis=0)

    def fill(s, second):
        more = pair_forcing(s, left_ref, right_ref, picks, flux[s], force)
        forcing_ref[s] = pltpu.roll(more, 2 * PITCH - reach, 1)
        odd_ref[s] = (pair_rows(center_ref[2 * s], second, reach) + more).astype(BF)

    def fill_pair(s, carry):
        fill(s, center_ref[2 * s + 1])
        return carry

    def join(s, carry):
        even_ref[s] = jnp.concatenate([odd_ref[s][:, PITCH:], odd_ref[s + 1][:, :PITCH]], axis=1)
        return carry

    lax.fori_loop(0, own_pairs - 1, fill_pair, 0)
    fill(own_pairs - 1, center_ref[rows - 1])
    lax.fori_loop(0, own_pairs - 1, join, 0)
    even_ref[own_pairs - 1] = odd_ref[own_pairs - 1]
    for at, ref in ((0, first_ref), (rows - reach, last_ref)):
        for d in range(reach):
            half = (at + d) % 2
            ref[d] = odd_ref[(at + d) // 2][:, half * PITCH : (half + 1) * PITCH]


def wet_rows(at, center, picks, parts, force, reach):
    rows, ch, _ = center.shape
    edge = jax.ShapeDtypeStruct((reach, ch, PITCH), BF)
    pairs = (rows + 1) // 2
    own = jax.ShapeDtypeStruct((pairs, ch, 2 * PITCH), BF)
    return pl.pallas_call(
        functools.partial(wet_kernel, reach),
        out_shape=(own, own, jax.ShapeDtypeStruct(own.shape, F32), edge, edge),
        in_specs=[SMEM] + [VMEM] * 4,
        out_specs=(VMEM,) * 5,
        scratch_shapes=[
            pltpu.VMEM((pairs, 4, 2 * PITCH), F32),
            pltpu.VMEM((pairs, 8, ch), F32),
            pltpu.VMEM((pairs, 8, ch), F32),
        ],
        compiler_params=pltpu.CompilerParams(vmem_limit_bytes=24 << 20),
        cost_estimate=pl.CostEstimate(flops=1 << 20, bytes_accessed=1 << 20, transcendentals=0),
        name="wet_rows",
    )(at, center, picks, parts, force)


def ocean_kernel(
    reach, mask_tiles, center_ref, forcing_ref, odd_ref, even_ref, low_ref, high_ref, taps_ref, gain_ref,
    expand_ref, contract_ref, mask_ref, out_ref, odd, even, taps, gain, flag, smooth
):
    step = pl.program_id(0)
    _, ch, cols = center_ref.shape
    high_ch, wide = even.shape[1:]
    pairs = smooth.shape[0]
    side = 2 * reach + 1
    own_pairs = odd_ref.shape[0]

    @pl.when(step == 0)
    def _():
        def widen(s, carry):
            odd[s + 2, :ch, :] = odd_ref[s].astype(F32)
            even[s + 2, :ch, :] = even_ref[s].astype(F32)
            return carry

        lax.fori_loop(0, own_pairs, widen, 0)
        odd[0, :ch, PITCH:] = low_ref[0].astype(F32)
        odd[1, :ch, :] = jnp.concatenate([low_ref[1].astype(F32), low_ref[2].astype(F32)], axis=1)
        odd[own_pairs + 1, :ch, PITCH:] = high_ref[0].astype(F32)
        odd[own_pairs + 2, :ch, :] = jnp.concatenate(
            [high_ref[1].astype(F32), high_ref[2].astype(F32)], axis=1
        )
        for t in (0, 1, own_pairs + 1, own_pairs + 2):
            even[t] = jnp.concatenate([odd[t][:, PITCH:], odd[t + 1][:, :PITCH]], axis=1)
        for k in range(side * side):
            taps[k] = jnp.broadcast_to(taps_ref[:, k : k + 1], taps.shape[1:])
        gain[...] = jnp.broadcast_to(gain_ref[...], gain.shape)
        tall, across = mask_tiles
        mask = mask_ref[...].astype(F32).astype(BF)
        spread = 0.0
        for half in range(2):
            pair = lax.broadcasted_iota(jnp.int32, (32, 8), 0)
            tile = lax.broadcasted_iota(jnp.int32, (32, 8), 1)
            up = ((2 * pair + half) // tall == tile).astype(F32).astype(BF)
            lane = lax.broadcasted_iota(jnp.int32, (8, wide), 1) - half * PITCH
            tile = lax.broadcasted_iota(jnp.int32, (8, wide), 0)
            side_by = (lane >= 0) & (lane < cols) & (lane // across == tile)
            side_by = side_by.astype(F32).astype(BF)
            spread = spread + dot(dot(up, mask).astype(BF), side_by)
        for s in range(flag.shape[0]):
            flag[s] = jnp.broadcast_to(spread[s : s + 1, :], (8, wide))

    start = step * pairs

    def channels(c, carry):
        at = pl.multiple_of(c * 8, 8)
        total = [None] * pairs
        for dx in range(side):
            part = [None] * pairs
            for dy in range(side):
                tap = taps[dy * side + dx, pl.ds(at, 8), :]
                tap = jnp.concatenate([tap] * (wide // 128), axis=1)
                for p in range(pairs):
                    if dy % 2 == 0:
                        value = even[start + p + dy // 2, pl.ds(at, 8), :]
                    else:
                        value = odd[start + p + dy // 2 + 1, pl.ds(at, 8), :]
                    term = tap * value
                    part[p] = term if part[p] is None else part[p] + term
            for p in range(pairs):
                moved = part[p] if dx == 0 else pltpu.roll(part[p], wide - dx, 1)
                total[p] = moved if total[p] is None else total[p] + moved
        for p in range(pairs):
            smooth[p, pl.ds(at, 8), :] = total[p]
        return carry

    lax.fori_loop(0, high_ch // 8, channels, 0)
    scale = jnp.concatenate([gain[...]] * (wide // 128), axis=1)
    for p in range(pairs):
        value = smooth[p, :ch, :]
        value = value - jnp.mean(value, axis=0, keepdims=True)
        spread = jnp.mean(value * value, axis=0, keepdims=True)
        normed = (value * lax.rsqrt(spread + 1e-06) * scale).astype(BF)
        hidden = dot(expand_ref[...], normed)
        inner = hidden * (0.7978845608028654 + 0.035677408136300125 * (hidden * hidden))
        hidden = (hidden + hidden * jnp.tanh(inner)).astype(BF)
        branch = 0.5 * dot(contract_ref[...], hidden)
        change = flag[start + p][:1] * (forcing_ref[p] + branch)
        for half in range(2):
            moved = change[:, half * PITCH : half * PITCH + cols]
            out_ref[2 * p + half] = (center_ref[2 * p + half].astype(F32) + moved).astype(BF)


def ocean_block(
    center, forcing, odd, even, low, high, taps, gain, expand, contract, mask, mask_tiles, reach
):
    rows, ch, cols = center.shape
    pairs = 6
    steps = pl.cdiv((rows + 1) // 2, pairs)
    high_ch = pl.cdiv(ch, 8) * 8
    deep = steps * pairs + reach + 1
    whole = lambda a: pl.BlockSpec(a.shape, lambda g: (0,) * a.ndim)
    operands = (center, forcing, odd, even, low, high, taps, gain, expand, contract, mask)
    return pl.pallas_call(
        functools.partial(ocean_kernel, reach, mask_tiles),
        out_shape=jax.ShapeDtypeStruct(center.shape, BF),
        grid=(steps,),
        in_specs=[
            pl.BlockSpec((2 * pairs, ch, cols), lambda g: (g, 0, 0)),
            pl.BlockSpec((pairs, ch, 2 * PITCH), lambda g: (g, 0, 0)),
            *(whole(a) for a in operands[2:]),
        ],
        out_specs=pl.BlockSpec((2 * pairs, ch, cols), lambda g: (g, 0, 0)),
        scratch_shapes=[
            pltpu.VMEM((deep, high_ch, 2 * PITCH), F32),
            pltpu.VMEM((deep, high_ch, 2 * PITCH), F32),
            pltpu.VMEM((taps.shape[1], high_ch, 128), F32),
            pltpu.VMEM((ch, 128), F32),
            pltpu.VMEM((steps * pairs, 8, 2 * PITCH), F32),
            pltpu.VMEM((pairs, high_ch, 2 * PITCH), F32),
        ],
        compiler_params=pltpu.CompilerParams(vmem_limit_bytes=32 << 20),
        cost_estimate=pl.CostEstimate(
            flops=30 << 30, bytes_accessed=8 << 20, transcendentals=3 << 20
        ),
        name="ocean_block",
    )(*operands)


def shift(first, last, axis):
    count = lax.axis_size(axis)
    up = [(i, i + 1) for i in range(count - 1)]
    down = [(target, source) for source, target in up]
    return lax.ppermute(last, axis, up), lax.ppermute(first, axis, down)


def body(
    atmos,
    sea_temp_gain,
    legendre_analysis,
    legendre_synthesis,
    spectral_mixing_weight,
    surface_flux_weight,
    flux_ocean_forcing,
    ocean,
    ocean_tile_mask,
    depthwise_filter,
    norm_gain_vector,
    expand_matrix,
    contract_matrix,
):
    lat_parts = lax.axis_size("lat")
    chan_parts = lax.axis_size("chan")
    chan_at = lax.axis_index("chan")
    ch, rows, lon = atmos.shape
    per_dev, degrees, _ = legendre_analysis.shape
    ocean_ch, _, cols = ocean.shape
    reach = depthwise_filter.shape[2] // 2
    peers = lat_parts * chan_parts
    padded_rows = 2 * HALF

    table_fwd, table_inv = dft_tables(lon, peer_modes(lat_parts, chan_parts, per_dev))
    table_fwd, table_inv = jnp.asarray(table_fwd), jnp.asarray(table_inv)
    swap_out = jnp.asarray(row_swap(16, HALF))
    swap_in = jnp.asarray(row_swap(HALF, 16))

    x = jnp.transpose(atmos, (1, 0, 2))
    sea = jnp.transpose(ocean, (1, 0, 2))

    def exchange(wire):
        return lax.all_to_all(
            wire.reshape(peers, HALF, 8 * ch), ("chan", "lat"), 0, 0, tiled=True
        ).reshape(wire.shape)

    at = jnp.reshape(chan_at, (1,)).astype(jnp.int32)
    parts = flux_parts(at, x, sea, surface_flux_weight, reach, chan_parts)
    parts = lax.all_to_all(parts, "chan", 0, 0, tiled=True)

    gain = sea_temp_gain[None]
    wire = forward(at, x, sea, gain, table_fwd, swap_out)
    gathered = exchange(wire)
    sea, legendre_analysis, legendre_synthesis, wire = lax.optimization_barrier(
        (sea, legendre_analysis, legendre_synthesis, wire)
    )
    force = flux_ocean_forcing.T
    force_high = force.astype(BF)
    force_low = (force - force_high.astype(F32)).astype(BF)
    force = jnp.concatenate([force_high, force_high, force_low, jnp.zeros_like(force_low)], axis=0)
    picks = jnp.asarray(edge_picks(reach, cols + 2 * reach))
    odd, even, forcing, first, last = wet_rows(at, sea, picks, parts, force, reach)
    low, high = shift(first, last, "lat")

    def banded(table):
        table = table.reshape(per_dev, lat_parts, rows, degrees)
        table = jnp.pad(table, ((0, 0), (0, 0), (0, padded_rows - rows), (0, 0)))
        table = table.reshape(per_dev, lat_parts, HALF, 2, degrees).transpose(0, 3, 1, 2, 4)
        return table.reshape(per_dev, 2, lat_parts * HALF, degrees)

    analysis = banded(jnp.transpose(legendre_analysis, (0, 2, 1)))
    synthesis = banded(legendre_synthesis)
    analysis, first, last = lax.optimization_barrier((analysis, first, last))
    back = spectral(
        gathered, analysis, synthesis, spectral_mixing_weight, jnp.asarray(spread_last(lat_parts))
    )
    back, low, high = lax.optimization_barrier((back, low, high))
    returned = exchange(back)

    tile_rows, tile_cols = ocean_tile_mask.shape
    mask = jnp.pad(ocean_tile_mask, ((0, 8 - tile_rows), (0, 8 - tile_cols)))
    taps = depthwise_filter.reshape(ocean_ch, -1).astype(F32)
    taps = jnp.pad(taps, ((0, -ocean_ch % 8), (0, 0)))
    ocean_next = ocean_block(
        sea,
        forcing,
        odd,
        even,
        low,
        high,
        taps,
        norm_gain_vector[:, None],
        expand_matrix,
        contract_matrix,
        mask,
        (rows // tile_rows, cols // tile_cols),
        reach,
    )

    atmos_next = inverse(returned, table_inv, swap_in, x, gain, parts)
    return (jnp.transpose(atmos_next, (1, 0, 2)), jnp.transpose(ocean_next, (1, 0, 2)))


def solution(mesh):
    in_specs = (
        P("chan", "lat", None),
        P("chan"),
        P(("lat", "chan"), None, None),
        P(("lat", "chan"), None, None),
        P(),
        P(None, "chan"),
        P(),
        P(None, "lat", "chan"),
        P("lat", "chan"),
        P(),
        P(),
        P(),
        P(),
    )
    out_specs = (P("chan", "lat", None), P(None, "lat", "chan"))
    return jax.shard_map(body, mesh=mesh, in_specs=in_specs, out_specs=out_specs, check_vma=False)
```
